128 devices in a mesh: lon: 16 (over y_hi, z, core), lat: 8 (over y_lo, x).
Axes of the slice: x: 4, y: 4 (y_hi: 2, y_lo: 2; y = y_hi * 2 + y_lo), z: 4, core: 2. Of those that a mesh axis runs over, the one named last changes fastest.
Arguments:
- fine_tokens: bfloat16 [2, 96, 768, 192], P(None, 'lat', 'lon'), may hold values from -6 to 6
- cotangent: bfloat16 [2, 48, 384, 384], P(None, 'lat', 'lon'), may hold values from -6 to 6
- fine_gain: float32 [192], replicated, may hold values from 0.25 to 1.75
- fine_project: bfloat16 [192, 576], replicated, may hold values from -0.4375 to 0.4375
- fine_combine: bfloat16 [192, 192], replicated, may hold values from -0.4375 to 0.4375
- fine_table: float32 [1, 16, 3312, 6], P(None, 'lat'), may hold values from -2 to 303
- fine_types: float32 [3, 6], replicated, may hold values from -3 to 3
- merge_gain: float32 [768], replicated, may hold values from 0.25 to 1.75
- merge_weight: bfloat16 [768, 384], replicated, may hold values from -0.21875 to 0.21875
- coarse_gain: float32 [384], replicated, may hold values from 0.25 to 1.75
- coarse_project: bfloat16 [384, 1152], replicated, may hold values from -0.3125 to 0.3125
- coarse_combine: bfloat16 [384, 384], replicated, may hold values from -0.3125 to 0.3125
- coarse_table: float32 [1, 8, 3312, 12], P(None, 'lat'), may hold values from -2 to 303
- coarse_types: float32 [3, 12], replicated, may hold values from -3 to 3
- surface_type: int32 [96, 768], replicated, may hold values from 0 to 2
- latitude_valid: int32 [96], replicated, may hold values from 0 to 1, as said below
- bias_index: int32 [144, 144], replicated, may hold values from 0 to 3311
Outputs:
- coarse_tokens: bfloat16 [2, 48, 384, 384], P(None, 'lat', 'lon')
- tokens_gradient: bfloat16 [2, 96, 768, 192], P(None, 'lat', 'lon')
- fine_project_gradient: float32 [192, 576], replicated
- fine_combine_gradient: float32 [192, 192], replicated
- merge_gradient: float32 [768, 384], replicated
- coarse_project_gradient: float32 [384, 1152], replicated
- coarse_combine_gradient: float32 [384, 384], replicated
The draws below stay inside these ranges and needn't reach their ends.
Inputs may be any that keep to these rules, and one draw needn't show every extreme that they name: `latitude_valid`: exactly 6 entries are 0: a run at the start and a run at the end, either of which may be empty.
All inputs are finite; a program needn't handle non-finite values.
Results may differ from the reference program's by a relative error of at most 0.035.
Values may be sent and summed in bfloat16 or wider, within the bound.
No kernel may reach another device: no remote copies, remote signals or barrier semaphores. Data moves between devices by JAX's collectives and lax.ppermute only.
A program may use at most 128 MiB of HBM per device.

```python
import math
from functools import partial
import jax
import jax.numpy as jnp
from jax import lax

LEV = 2
H1 = 6
H2 = 12
D1 = 192
D2 = 384
NPOS = 3312
NLAT = 96
NLON = 768
LEVWIN = 1
PAD_ROWS = 6


def drawn_table(key, table_shape):
    return jnp.clip(0.5 * jax.random.normal(key, table_shape, jnp.float32), -2.0, 2.0)


def draw_fine_table(key, part):
    key = jax.random.fold_in(key, 11)
    table_shape = (LEVWIN, NLAT // 6, NPOS, H1)
    return drawn_table(key, table_shape)


def draw_coarse_table(key, part):
    key = jax.random.fold_in(key, 13)
    table_shape = (LEVWIN, NLAT // 12, NPOS, H2)
    return drawn_table(key, table_shape)


def draw_latitude_valid(key, part):
    key = jax.random.fold_in(key, 17)
    north_rows = jax.random.randint(key, (), 0, PAD_ROWS + 1)
    positions = jnp.arange(NLAT, dtype=jnp.int32)
    return ((positions >= north_rows) & (positions < NLAT - PAD_ROWS + north_rows)).astype(jnp.int32)


def touch_ends(array, stream_key, low, largest):
    longest = array.shape.index(max(array.shape))
    spots = []
    for shift in (0, 1):
        where = [jax.random.randint(jax.random.fold_in(stream_key, axis), (), 0, length) for axis, length in enumerate(array.shape)]
        where[longest] = (where[longest] + shift) % array.shape[longest]
        spots.append(tuple(where))
    return array.at[spots[0]].set(low).at[spots[1]].set(largest)


def level_of(stream_key, extent, cuts, smallest, high):
    level = 1.0
    for position, blocks in cuts:
        heights = jax.random.uniform(jax.random.fold_in(jax.random.fold_in(stream_key, 6), position), (blocks,), jnp.float32, smallest / len(cuts), high / len(cuts))
        level = level * jnp.repeat(jnp.exp(heights), extent[position] // blocks).reshape((-1,) + (1,) * (len(extent) - 1 - position))
    return level


def normal_values(stream_key, dims, scale, most, cuts=(), kind=jnp.bfloat16):
    array = scale * jax.random.normal(stream_key, dims, jnp.float32)
    if cuts:
        array = array * level_of(stream_key, dims, cuts, -0.22, 0.18)
    return jnp.clip(array, -most, most).astype(kind)


def setup_inputs(seed: int = 0) -> dict:
    key_list = jax.random.split(jax.random.key(seed), 18)
    return {
        "fine_tokens": normal_values(key_list[0], (LEV, NLAT, NLON, D1), 1.0, 6.0, ((1, 8), (2, 16))),
        "cotangent": normal_values(key_list[1], (LEV, NLAT // 2, NLON // 2, D2), 1.0, 6.0, ((1, 8), (2, 16))),
        "fine_gain": jnp.clip(1.0 + 0.15 * jax.random.normal(key_list[2], (D1,), jnp.float32), 0.25, 1.75),
        "fine_project": normal_values(key_list[3], (D1, 3 * D1), D1 ** -0.5, 0.4375),
        "fine_combine": normal_values(key_list[4], (D1, D1), D1 ** -0.5, 0.4375),
        "fine_table": draw_fine_table(jax.random.fold_in(key_list[17], 71), 0),
        "fine_types": normal_values(key_list[6], (3, H1), 1.0, 3.0, (), jnp.float32),
        "merge_gain": jnp.clip(1.0 + 0.15 * jax.random.normal(key_list[7], (4 * D1,), jnp.float32), 0.25, 1.75),
        "merge_weight": normal_values(key_list[8], (4 * D1, D2), (4 * D1) ** -0.5, 0.21875),
        "coarse_gain": jnp.clip(1.0 + 0.15 * jax.random.normal(key_list[9], (D2,), jnp.float32), 0.25, 1.75),
        "coarse_project": normal_values(key_list[10], (D2, 3 * D2), D2 ** -0.5, 0.3125),
        "coarse_combine": normal_values(key_list[11], (D2, D2), D2 ** -0.5, 0.3125),
        "coarse_table": draw_coarse_table(jax.random.fold_in(key_list[17], 71), 0),
        "coarse_types": normal_values(key_list[13], (3, H2), 1.0, 3.0, (), jnp.float32),
        "surface_type": touch_ends(jax.random.randint(key_list[14], (NLAT, NLON), 0, 3), jax.random.fold_in(key_list[14], 1), 0, 2).astype(jnp.int32),
        "latitude_valid": draw_latitude_valid(jax.random.fold_in(key_list[17], 71), 0),
        "bias_index": touch_ends(jax.random.randint(key_list[16], (144, 144), 0, NPOS), jax.random.fold_in(key_list[16], 1), 0, NPOS - 1).astype(jnp.int32),
    }


EPSILON = 1e-05

def normalize(tokens, gain_vector):
    values = tokens.astype(jnp.float32)
    average = lax.optimization_barrier(jnp.mean(values, axis=-1, keepdims=True))
    centred = values - average
    spread = lax.optimization_barrier(jnp.mean(centred * centred, axis=-1, keepdims=True))
    return (centred * lax.rsqrt(spread + EPSILON) * gain_vector).astype(jnp.bfloat16)

def merge_norm(tokens, gain_vector):
    levels, row_count, column_count, channels = tokens.shape
    merged = tokens.reshape(levels, row_count // 2, 2, column_count // 2, 2, channels)
    merged = merged.transpose(0, 1, 3, 2, 4, 5).reshape(levels, row_count // 2, column_count // 2, 4 * channels)
    return normalize(merged, gain_vector)

def surface_codes(surface_type, latitude_valid, stride):
    if stride == 1:
        surface = surface_type
        valid_rows = latitude_valid
    else:
        surface = surface_type[::2, ::2]
        valid_rows = jnp.maximum(latitude_valid[0::2], latitude_valid[1::2])
    return (jnp.roll(surface, (-3, -6), (0, 1)), jnp.roll(valid_rows, -3))

def contract(left, right):
    return lax.dot_general(left.reshape(-1, left.shape[-1]), right.reshape(-1, right.shape[-1]), (((0,), (0,)), ((), ())), preferred_element_type=jnp.float32)

def attend(triple, bias_table, type_bias, bias_index, surface, valid_rows, wrap_rows, head_count):
    levels, row_count, column_count, triple_width = triple.shape
    channels = triple_width // 3
    head_size = channels // head_count
    level_windows, row_windows, column_windows = (levels // 2, row_count // 6, column_count // 12)
    blocks = triple.reshape(level_windows, 2, row_windows, 6, column_windows, 12, 3, head_count, head_size)
    blocks = blocks.transpose(2, 6, 0, 4, 7, 1, 3, 5, 8).reshape(row_windows, 3, level_windows, column_windows, head_count, 144, head_size)
    key_kinds = surface.reshape(row_windows, 6, column_windows, 12).transpose(0, 2, 1, 3)
    key_kinds = jnp.broadcast_to(key_kinds.reshape(row_windows, column_windows, 1, 72), (row_windows, column_windows, 2, 72)).reshape(row_windows, column_windows, 144)
    valid_tokens = jnp.broadcast_to(valid_rows.reshape(row_windows, 1, 6, 1), (row_windows, 2, 6, 12)).reshape(row_windows, 144) == 1
    wrap_tokens = jnp.broadcast_to(wrap_rows.reshape(row_windows, 1, 6, 1), (row_windows, 2, 6, 12)).reshape(row_windows, 144)
    level_flag = jnp.broadcast_to((jnp.arange(levels) >= levels - 1).reshape(level_windows, 2, 1), (level_windows, 2, 72)).reshape(level_windows, 144)
    same_level = level_flag[:, :, None] == level_flag[:, None, :]
    diagonal = jnp.eye(144, dtype=bool)
    tables = jnp.moveaxis(bias_table, 1, 0)
    score_scale = head_size ** (-0.5)

    def one_row(inputs):
        window_block, table_rows, kinds_here, valid_keys, wrap_flags = inputs
        queries, key_block, value_block = (window_block[0], window_block[1], window_block[2])
        scores = jnp.einsum('lchqd,lchkd->lchqk', queries.astype(jnp.float32), key_block.astype(jnp.float32))
        positional = jnp.take(table_rows, bias_index.reshape(-1), axis=1)
        positional = positional.reshape(level_windows, 144, 144, head_count).transpose(0, 3, 1, 2)
        one_hot = (kinds_here[..., None] == jnp.arange(3)).astype(jnp.float32)
        type_term = lax.optimization_barrier(jnp.sum(one_hot[..., None] * type_bias, axis=2)).transpose(0, 2, 1)
        scores = scores * score_scale + positional[:, None] + type_term[None, :, :, None, :]
        keep_pairs = (wrap_flags[:, None] == wrap_flags[None, :]) & (valid_keys[None, :] | diagonal)
        allowed = same_level & keep_pairs[None]
        scores = jnp.where(allowed[:, None, None], scores, -jnp.inf)
        row_top = lax.stop_gradient(lax.optimization_barrier(jnp.max(scores, axis=-1, keepdims=True)))
        weights = jnp.exp(scores - row_top)
        weights = (weights / lax.optimization_barrier(jnp.sum(weights, axis=-1, keepdims=True))).astype(jnp.bfloat16)
        mixture = jnp.einsum('lchqk,lchkd->lchqd', weights.astype(jnp.float32), value_block.astype(jnp.float32))
        return mixture.astype(jnp.bfloat16)
    mixture = lax.map(one_row, (blocks, tables, key_kinds, valid_tokens, wrap_tokens))
    mixture = mixture.reshape(row_windows, level_windows, column_windows, head_count, 2, 6, 12, head_size)
    return mixture.transpose(1, 4, 0, 5, 2, 6, 3, 7).reshape(levels, row_count, column_count, channels)

def roll_forward(values):
    return jnp.roll(values, (-1, -3, -6), (0, 1, 2))

def roll_backward(values):
    return jnp.roll(values, (1, 3, 6), (0, 1, 2))

def level_forward(tokens, gain_vector, project, combine, attention):
    normed = normalize(tokens, gain_vector)
    rolled = roll_forward(normed)
    triple = jnp.dot(rolled, project, preferred_element_type=jnp.float32).astype(jnp.bfloat16)
    restored = roll_backward(attention(triple))
    output = tokens.astype(jnp.float32) + jnp.dot(restored, combine, preferred_element_type=jnp.float32)
    return (output.astype(jnp.bfloat16), (rolled, triple, restored))

def level_backward(tokens, gain_vector, project, combine, attention, kept_arrays, delta_output):
    rolled, triple, restored = kept_arrays
    delta_restored = jnp.dot(delta_output, combine.T, preferred_element_type=jnp.float32).astype(jnp.bfloat16)
    combine_gradient = contract(restored, delta_output)
    attended, attention_pullback = jax.vjp(attention, triple)
    delta_triple = attention_pullback(roll_forward(delta_restored))[0]
    project_gradient = contract(rolled, delta_triple)
    delta_rolled = jnp.dot(delta_triple, project.T, preferred_element_type=jnp.float32).astype(jnp.bfloat16)
    delta_normed = roll_backward(delta_rolled)
    normed, norm_pullback = jax.vjp(lambda values: normalize(values, gain_vector), tokens)
    return (delta_output + norm_pullback(delta_normed)[0], project_gradient, combine_gradient)

def local_attention(stride, bias_table, type_bias, head_count, surface_type, latitude_valid, bias_index, row_count):
    surface, valid_rows = surface_codes(surface_type, latitude_valid, stride)
    wrap_rows = jnp.arange(row_count) >= row_count - 3
    return partial(attend, bias_table=bias_table, type_bias=type_bias, bias_index=bias_index, surface=surface, valid_rows=valid_rows, wrap_rows=wrap_rows, head_count=head_count)

def reference(fine_tokens, cotangent, fine_gain, fine_project, fine_combine, fine_table, fine_types, merge_gain, merge_weight, coarse_gain, coarse_project, coarse_combine, coarse_table, coarse_types, surface_type, latitude_valid, bias_index):
    fine_attention = local_attention(1, fine_table, fine_types, H1, surface_type, latitude_valid, bias_index, fine_tokens.shape[1])
    fine_output, fine_kept = level_forward(fine_tokens, fine_gain, fine_project, fine_combine, fine_attention)
    merged = merge_norm(fine_output, merge_gain)
    coarse_input = jnp.dot(merged, merge_weight, preferred_element_type=jnp.float32).astype(jnp.bfloat16)
    coarse_attention = local_attention(2, coarse_table, coarse_types, H2, surface_type, latitude_valid, bias_index, coarse_input.shape[1])
    coarse_output, coarse_kept = level_forward(coarse_input, coarse_gain, coarse_project, coarse_combine, coarse_attention)
    delta_coarse, coarse_project_sum, coarse_combine_sum = level_backward(coarse_input, coarse_gain, coarse_project, coarse_combine, coarse_attention, coarse_kept, cotangent)
    merge_sum = contract(merged, delta_coarse)
    delta_merged = jnp.dot(delta_coarse, merge_weight.T, preferred_element_type=jnp.float32).astype(jnp.bfloat16)
    merged_again, merge_pullback = jax.vjp(lambda values: merge_norm(values, merge_gain), fine_output)
    delta_fine = merge_pullback(delta_merged)[0]
    tokens_gradient, fine_project_sum, fine_combine_sum = level_backward(fine_tokens, fine_gain, fine_project, fine_combine, fine_attention, fine_kept, delta_fine)
    fine_count = fine_tokens.shape[0] * fine_tokens.shape[1] * fine_tokens.shape[2]
    fine_scale = 1.0 / math.sqrt(fine_count)
    coarse_scale = 1.0 / math.sqrt(fine_count // 4)
    return (coarse_output, tokens_gradient, fine_project_sum * fine_scale, fine_combine_sum * fine_scale, merge_sum * coarse_scale, coarse_project_sum * coarse_scale, coarse_combine_sum * coarse_scale)
```

```python
import math
from functools import partial

import numpy as np
import jax
import jax.numpy as jnp
from jax import lax
from jax.experimental import pallas as pl
from jax.experimental.pallas import tpu as pltpu
from jax.sharding import PartitionSpec as P

F32 = jnp.float32
BF16 = jnp.bfloat16
EPSILON = 1e-05
HEAD = 32
SCALE = HEAD ** (-0.5)
BLOCKED = -1e30
NT = (((1,), (1,)), ((), ()))
TN = (((0,), (0,)), ((), ()))
NN = (((1,), (0,)), ((), ()))


def pad16(n):
    return (n + 15) // 16 * 16


class Shift:
    def __init__(self, rows, cols, dr, dc, source, target, forward):
        if forward:
            ranges = (
                (range(0, dr), range(dc, cols)),
                (range(dr, rows), range(0, dc)),
                (range(0, dr), range(0, dc)),
            )
        else:
            ranges = (
                (range(rows - dr, rows), range(0, cols - dc)),
                (range(0, rows - dr), range(cols - dc, cols)),
                (range(rows - dr, rows), range(cols - dc, cols)),
            )
        lists = [[(r, c) for r in rr for c in cc] for rr, cc in ranges]
        self.sizes = [pad16(len(x)) for x in lists]
        self.own = rows * cols
        send = []
        for x, size in zip(lists, self.sizes):
            send += [source(r, c) for r, c in x] + [0] * (size - len(x))
        self.send = np.array(send, np.int32)[:, None]
        offsets = [self.own, self.own + self.sizes[0], self.own + self.sizes[0] + self.sizes[1]]
        places = [{rc: o + n for n, rc in enumerate(x)} for x, o in zip(lists, offsets)]
        take = np.zeros((self.own, 1), np.int32)
        sign = 1 if forward else -1
        for r in range(rows):
            for c in range(cols):
                a, b = r + sign * dr, c + sign * dc
                out_row, out_col = not 0 <= a < rows, not 0 <= b < cols
                a, b = a % rows, b % cols
                if out_row or out_col:
                    which = 2 if out_row and out_col else (0 if out_row else 1)
                    place = places[which][(a, b)]
                else:
                    place = source(a, b)
                take[target(r, c), 0] = place
        self.take = take
        self.total = self.own + sum(self.sizes)


def pad8(n):
    return (n + 7) // 8 * 8


def raster(cols):
    return lambda r, c: r * cols + c


def windowed(cols):
    per_row = cols // 12
    return lambda r, c: ((r // 6) * per_row + c // 12) * 72 + (r % 6) * 12 + c % 12


def merging(cols):
    coarse = windowed(cols // 2)
    quarter = lambda rows: rows
    return lambda r, c: ((r % 2) * 2 + c % 2) * 144 + coarse(r // 2, c // 2)


def one_hot(index, width):
    lanes = lax.broadcasted_iota(jnp.int32, (index.shape[0], width), 1)
    return jnp.where(lanes == index, 1.0, 0.0).astype(BF16)


def mm(a, b, dims=NN):
    return lax.dot_general(a, b, dims, preferred_element_type=F32)


def round16(x):
    return x.astype(BF16).astype(F32)


def pick(take, total, own, parts):
    return mm(one_hot(take, total), jnp.concatenate([own] + parts, axis=0))


def head_masks(channels):
    lanes = lax.broadcasted_iota(jnp.int32, (1, channels), 1)
    return [
        jnp.where((lanes >= HEAD * h) & (lanes < HEAD * (h + 1)), 1.0, 0.0)
        for h in range(channels // HEAD)
    ]


def spread_heads(x, masks):
    return jnp.concatenate([x * m for m in masks], axis=0).astype(BF16)


def fold_heads(x, masks):
    out = x[0:72] * masks[0]
    for h in range(1, len(masks)):
        out = out + x[72 * h : 72 * (h + 1)] * masks[h]
    return out


def weights_of(k16, qbig, kinds16, types16, bias):
    x = mm(k16, qbig, NT) * SCALE + (mm(kinds16, types16, NT) + bias)
    e = jnp.exp(x - jnp.max(x, axis=0, keepdims=True))
    return (e * (1.0 / jnp.sum(e, axis=0, keepdims=True))).astype(BF16)


def attention_back(q, k, v, p16, do, masks):
    k16 = k.astype(BF16)
    dobig = spread_heads(do, masks)
    qbig = spread_heads(q, masks)
    p = p16.astype(F32)
    dv = mm(p16, dobig)
    dp = round16(mm(v.astype(BF16), dobig, NT))
    pd = p * dp
    ds = ((pd - p * jnp.sum(pd, axis=0, keepdims=True)) * SCALE).astype(BF16)
    dq = fold_heads(mm(ds, k16, TN), masks)
    dk = mm(ds, qbig)
    return dq, dk, dv


def moments(parts):
    count = sum(x.shape[-1] for x in parts)
    mean = sum(jnp.sum(x, axis=-1, keepdims=True) for x in parts) * (1.0 / count)
    centred = [x - mean for x in parts]
    spread = sum(jnp.sum(c * c, axis=-1, keepdims=True) for c in centred) * (1.0 / count)
    return centred, lax.rsqrt(spread + EPSILON)


def norm_back(centred, inverse, gains, deltas):
    count = sum(x.shape[-1] for x in centred)
    scaled = [d * g for d, g in zip(deltas, gains)]
    unit = [c * inverse for c in centred]
    mean = sum(jnp.sum(s, axis=-1, keepdims=True) for s in scaled) * (1.0 / count)
    along = sum(jnp.sum(s * u, axis=-1, keepdims=True) for s, u in zip(scaled, unit)) * (1.0 / count)
    return [(s - mean - u * along) * inverse for s, u in zip(scaled, unit)]


def send_out(index, own, refs, level):
    rows = mm(one_hot(index, own.shape[0]), own).astype(BF16)
    at = 0
    for ref in refs:
        n = ref.shape[1]
        ref[level] = rows[at : at + n]
        at += n


def prepare_kernel(fsel, csel, tokens, cot, fa, fb, fc, ca, cb, cc):
    nf, nc = tokens.shape[0] // 2, cot.shape[0] // 2
    for level in range(2):
        send_out(fsel[...], tokens[level * nf : (level + 1) * nf, :], (fa, fb, fc), level)
        send_out(csel[...], cot[level * nc : (level + 1) * nc, :], (ca, cb, cc), level)


def bias_kernel(
    level_rows, place, valid, index, table, surface, types, row, col,
    bias, kinds, typed, raw, parts,
):
    lat, lon, lats = place[0], place[1], place[2]
    windows, heads = bias.shape[1], bias.shape[3] // 72
    chunks = table.shape[1] // 128
    count = table.shape[0]
    pieces = [table[:, c * 128 : (c + 1) * 128] for c in range(chunks)]
    pad = [jnp.zeros((-count % 8, 128), F32)] if count % 8 else []
    whole = count + (-count % 8)
    high_part = jnp.concatenate([x for p in pieces for x in [round16(p)] + pad], axis=0)
    low_part = jnp.concatenate([x for p in pieces for x in [p - round16(p)] + pad], axis=0)
    parts[:, 0:128] = high_part.astype(BF16)
    parts[:, 128:256] = low_part.astype(BF16)
    lanes_down = lax.broadcasted_iota(jnp.int32, (128, 128), 0)

    def two_rows(i, carry):
        places = [index[2 * i + j] for j in range(2)]
        hot = jnp.concatenate(
            [jnp.where(lanes_down == (x & 127), 1.0, 0.0) for x in places], axis=1
        ).astype(BF16)
        found = mm(parts[...], jnp.concatenate([hot, hot], axis=0))
        for j in range(2):
            chunk = jnp.broadcast_to(places[j] >> 7, (8, 128))
            for g in range(0, whole, 8):
                total = jnp.zeros((8, 128), F32)
                for c in range(chunks):
                    at = c * whole + g
                    total = jnp.where(chunk == c, found[at : at + 8, 128 * j : 128 * (j + 1)], total)
                raw[pl.ds(g * 144 + 2 * i + j, 8, stride=144), :] = total
        return carry

    lax.fori_loop(0, 72, two_rows, 0, unroll=4)

    key = lax.broadcasted_iota(jnp.int32, (72, 72), 0)
    query = lax.broadcasted_iota(jnp.int32, (72, 72), 1)
    key_row = sum(jnp.where(key >= 12 * r, 1, 0) for r in range(1, 6))
    apart = jnp.where((key >= 36) != (query >= 36), 1, 0)
    rows, columns = surface.shape[0] // level_rows, surface.shape[1] // level_rows
    at_end = jnp.where(lat == lats - 1, 1, 0)
    for rw in range(windows):
        real = jnp.zeros((72, 72), jnp.int32)
        for r in range(6):
            spot = lax.rem(lat * (6 * windows) + (6 * rw + r + 3), rows) * level_rows
            here = valid[spot]
            for more in range(1, level_rows):
                here = jnp.maximum(here, valid[spot + more])
            real = jnp.where(key_row == r, here, real)
        good = (real == 1) | (key == query)
        if rw == windows - 1:
            good = good & (apart * at_end == 0)
        for level in range(2):
            for h in range(heads):
                at = (rw * heads + h) * 144 + level * 72
                bias[level, rw, :, 72 * h : 72 * (h + 1)] = jnp.where(
                    good, raw[at : at + 72, :][:, :72], BLOCKED
                )

    codes = surface[...].astype(F32).astype(BF16)
    tokens = kinds.shape[0]
    line = row[...] + lat * (6 * windows)
    line = jnp.where(line >= rows, line - rows, line) * level_rows
    spot = col[...] + lon * (12 * (tokens // 72 // windows))
    spot = jnp.where(spot >= columns, spot - columns, spot) * level_rows
    lines = mm(one_hot(line, surface.shape[0]), codes)
    lanes = lax.broadcasted_iota(jnp.int32, lines.shape, 1)
    code = jnp.sum(jnp.where(lanes == spot, lines, 0.0), axis=1, keepdims=True).astype(jnp.int32)
    lanes = lax.broadcasted_iota(jnp.int32, (tokens, 128), 1)
    kinds[...] = jnp.where((lanes == code) | (lanes == code + 3) | (lanes == code + 6), 1.0, 0.0)

    t = types[...]
    high = round16(t)
    middle = round16(t - high)
    lanes = lax.broadcasted_iota(jnp.int32, t.shape, 1)
    split = jnp.where(lanes < 3, high, jnp.where(lanes < 6, middle, t - high - middle))
    typed[...] = jnp.concatenate(
        [jnp.broadcast_to(split[h : h + 1], (72, 128)) for h in range(heads)], axis=0
    ).astype(BF16)


def fine_forward_kernel(
    take, sel, tokens, ra, rb, rc, gain, project, combine, bias, kinds, types,
    output, sa, sb, sc, kept_x, kept_p, kept_o,
    q_s, k_s, v_s, o_s,
):
    n = take.shape[0]
    width = tokens.shape[1]
    total = n + ra.shape[1] + rb.shape[1] + rc.shape[1]
    hot = one_hot(take[...], total)
    rolled = []
    for level in range(2):
        o = 1 - level
        source = jnp.concatenate([tokens[o * n : (o + 1) * n, :], ra[o], rb[o], rc[o]], axis=0)
        rolled.append(mm(hot, source))
    x = jnp.concatenate(rolled, axis=0)
    kept_x[...] = x.astype(BF16)
    (centred,), inverse = moments([x])
    u = (centred * inverse * gain[...]).astype(BF16)
    for i, scratch in enumerate((q_s, k_s, v_s)):
        scratch[...] = round16(mm(u, project[:, i * width : (i + 1) * width]))
    masks = head_masks(width)
    windows = n // 72
    across = windows // bias.shape[1]
    types16 = types[...]

    def window(w, carry):
        kinds16 = kinds[pl.ds(pl.multiple_of(w * 72, 8), 72), :].astype(BF16)
        for level in range(2):
            b = level * windows + w
            rows = pl.ds(pl.multiple_of(b * 72, 8), 72)
            qbig = spread_heads(q_s[rows, :], masks)
            p = weights_of(k_s[rows, :].astype(BF16), qbig, kinds16, types16, bias[level, w // across])
            kept_p[b] = p
            o_s[rows, :] = fold_heads(mm(p, v_s[rows, :].astype(BF16), TN), masks)
        return carry

    lax.fori_loop(0, windows, window, 0)
    o16 = o_s[...].astype(BF16)
    kept_o[...] = o16
    out = (x + mm(o16, combine[...])).astype(BF16)
    output[...] = out
    for level in range(2):
        send_out(sel[...], out[level * n : (level + 1) * n], (sa, sb, sc), level)


def coarse_kernel(
    take, ctake, csel, fsel, fine, ra, rb, rc, cot, da, db, dc,
    merge_gain, merge_weight, gain, project, combine, bias, kinds, types,
    output, oa, ob, oc, delta_fine, sa, sb, sc, gradients,
    q_s, k_s, v_s, o_s, do_s, dq_s, dk_s, dv_s, p_s,
):
    n = take.shape[0]
    quarter = n // 4
    thin = fine.shape[1]
    width = combine.shape[0]
    total = n + ra.shape[1] + rb.shape[1] + rc.shape[1]
    hot = one_hot(take[...], total)
    ctotal = quarter + da.shape[1] + db.shape[1] + dc.shape[1]
    chot = one_hot(ctake[...], ctotal)
    levels, cot_levels = [], []
    for level in range(2):
        source = jnp.concatenate([fine[level * n : (level + 1) * n, :], ra[level], rb[level], rc[level]], axis=0)
        levels.append(mm(hot, source))
        o = 1 - level
        source = jnp.concatenate([cot[o * quarter : (o + 1) * quarter, :], da[o], db[o], dc[o]], axis=0)
        cot_levels.append(mm(chot, source))
    cells = [
        jnp.concatenate([x[s * quarter : (s + 1) * quarter] for x in levels], axis=0) for s in range(4)
    ]
    d = jnp.concatenate(cot_levels, axis=0)
    d16 = d.astype(BF16)
    merge_gains = [merge_gain[s : s + 1, :] for s in range(4)]
    m_centred, m_inverse = moments(cells)
    merged = [(c * m_inverse * g).astype(BF16) for c, g in zip(m_centred, merge_gains)]
    weight = [merge_weight[s * thin : (s + 1) * thin, :] for s in range(4)]
    entered = sum(mm(a, w) for a, w in zip(merged, weight))
    x = round16(entered)
    (centred,), inverse = moments([x])
    u = (centred * inverse * gain[...]).astype(BF16)
    wq, wk, wv = (project[:, i * width : (i + 1) * width] for i in range(3))
    q_s[...] = round16(mm(u, wq))
    k_s[...] = round16(mm(u, wk))
    v_s[...] = round16(mm(u, wv))
    do_s[...] = round16(mm(d16, combine[...], NT))
    masks = head_masks(width)
    windows = quarter // 72
    types16 = types[...]

    def window(w, carry):
        kinds16 = kinds[pl.ds(pl.multiple_of(w * 72, 8), 72), :].astype(BF16)
        for level in range(2):
            rows = pl.ds(pl.multiple_of((level * windows + w) * 72, 8), 72)
            q, k, v = q_s[rows, :], k_s[rows, :], v_s[rows, :]
            p = weights_of(k.astype(BF16), spread_heads(q, masks), kinds16, types16, bias[level, 0])
            o_s[rows, :] = fold_heads(mm(p, v.astype(BF16), TN), masks)
            dq, dk, dv = attention_back(q, k, v, p, do_s[rows, :], masks)
            dq_s[rows, :] = dq
            dk_s[rows, :] = dk
            dv_s[rows, :] = dv
        return carry

    lax.fori_loop(0, windows, window, 0)
    o16 = o_s[...].astype(BF16)
    out = (x + mm(o16, combine[...])).astype(BF16)
    output[...] = out
    for level in range(2):
        send_out(csel[...], out[level * quarter : (level + 1) * quarter], (oa, ob, oc), level)
    dq16, dk16, dv16 = dq_s[...].astype(BF16), dk_s[...].astype(BF16), dv_s[...].astype(BF16)
    delta_rolled = round16(mm(dq16, wq, NT) + mm(dk16, wk, NT) + mm(dv16, wv, NT))
    (dx,) = norm_back([centred], inverse, [gain[...]], [delta_rolled])
    delta = (d + round16(dx)).astype(BF16)
    deltas = [round16(mm(delta, w, NT)) for w in weight]
    back = norm_back(m_centred, m_inverse, merge_gains, deltas)
    back = [b.astype(BF16) for b in back]
    for level in range(2):
        own = jnp.concatenate([b[level * quarter : (level + 1) * quarter] for b in back], axis=0)
        delta_fine[level * n : (level + 1) * n, :] = own
        send_out(fsel[...], own, (sa, sb, sc), level)
    sums = [jnp.concatenate([mm(m, delta, TN) for m in merged], axis=0)]
    sums += [mm(left, right, TN) for left, right in ((u, dq16), (u, dk16), (u, dv16), (o16, d16))]
    at = 0
    for block in sums:
        for j in range(width // 128):
            gradients[at : at + block.shape[0], :] = block[:, j * 128 : (j + 1) * 128].astype(BF16)
            at += block.shape[0]


def fine_backward_kernel(
    take, sel, own, ra, rb, rc, kept_x, kept_p, kept_o,
    gain, project, combine,
    output, sa, sb, sc, gradients,
    q_s, k_s, v_s, do_s, dq_s, dk_s, dv_s,
):
    n = take.shape[0]
    width = kept_x.shape[1]
    total = n + ra.shape[1] + rb.shape[1] + rc.shape[1]
    hot = one_hot(take[...], total)
    d = jnp.concatenate(
        [
            mm(hot, jnp.concatenate([own[l * n : (l + 1) * n, :], ra[l], rb[l], rc[l]], axis=0))
            for l in range(2)
        ],
        axis=0,
    )
    d16 = d.astype(BF16)
    do_s[...] = round16(mm(d16, combine[...], NT))
    (centred,), inverse = moments([kept_x[...].astype(F32)])
    u = (centred * inverse * gain[...]).astype(BF16)
    for i, scratch in enumerate((q_s, k_s, v_s)):
        scratch[...] = round16(mm(u, project[:, i * width : (i + 1) * width]))
    masks = head_masks(width)
    windows = n // 72

    def window(w, carry):
        for level in range(2):
            b = level * windows + w
            rows = pl.ds(pl.multiple_of(b * 72, 8), 72)
            dq, dk, dv = attention_back(
                q_s[rows, :], k_s[rows, :], v_s[rows, :], kept_p[b], do_s[rows, :], masks
            )
            dq_s[rows, :] = dq
            dk_s[rows, :] = dk
            dv_s[rows, :] = dv
        return carry

    lax.fori_loop(0, windows, window, 0)
    parts = [dq_s[...].astype(BF16), dk_s[...].astype(BF16), dv_s[...].astype(BF16)]
    delta_rolled = round16(
        sum(mm(a, project[:, i * width : (i + 1) * width], NT) for i, a in enumerate(parts))
    )
    (dx,) = norm_back([centred], inverse, [gain[...]], [delta_rolled])
    out = (d + round16(dx)).astype(BF16)
    output[...] = out
    for level in range(2):
        send_out(sel[...], out[level * n : (level + 1) * n], (sa, sb, sc), level)
    pieces = [mm(u, a, TN) for a in parts] + [mm(kept_o[...], d16, TN)]
    pieces = jnp.concatenate(pieces, axis=1).astype(BF16)
    for j in range(pieces.shape[1] // 128):
        gradients[j * width : (j + 1) * width, :] = pieces[:, j * 128 : (j + 1) * 128]


def restore_kernel(take, own, ra, rb, rc, output):
    n = take.shape[0]
    hot = one_hot(take[...], n + ra.shape[1] + rb.shape[1] + rc.shape[1])
    for level in range(2):
        o = 1 - level
        source = jnp.concatenate([own[o * n : (o + 1) * n, :], ra[o], rb[o], rc[o]], axis=0)
        output[level * n : (level + 1) * n, :] = mm(hot, source).astype(BF16)


VMEM = pl.BlockSpec(memory_space=pltpu.VMEM)
SMEM = pl.BlockSpec(memory_space=pltpu.SMEM)


def call(kernel, name, outs, scratch, args, smem=0, flops=10**9, limit=20):
    return pl.pallas_call(
        kernel,
        name=name,
        out_shape=[jax.ShapeDtypeStruct(s, d) for s, d in outs],
        in_specs=[SMEM] * smem + [VMEM] * (len(args) - smem),
        out_specs=[VMEM] * len(outs),
        scratch_shapes=[pltpu.VMEM(s, d) for s, d in scratch],
        cost_estimate=pl.CostEstimate(flops=flops, bytes_accessed=4 << 20, transcendentals=0),
        compiler_params=pltpu.CompilerParams(vmem_limit_bytes=limit << 20),
    )(*args)


def move(value, lat_step, lon_step):
    lons, lats = lax.axis_size("lon"), lax.axis_size("lat")
    if lat_step == 0:
        return lax.ppermute(value, "lon", [(s, (s + lon_step) % lons) for s in range(lons)])
    if lon_step == 0:
        return lax.ppermute(value, "lat", [(s, (s + lat_step) % lats) for s in range(lats)])
    pairs = [
        (a * lats + b, ((a + lon_step) % lons) * lats + (b + lat_step) % lats)
        for a in range(lons)
        for b in range(lats)
    ]
    return lax.ppermute(value, ("lon", "lat"), pairs)


def exchange(parts, step):
    a, b, c = parts
    return [move(a, step, 0), move(b, 0, step), move(c, step, step)]


def summed(blocks):
    count = lax.axis_size("lon") * lax.axis_size("lat")
    block = jnp.concatenate(blocks, axis=0)
    chunk = pad16(-(-block.shape[0] // count))
    block = jnp.pad(block, ((0, count * chunk - block.shape[0]), (0, 0))).reshape(count, chunk, 128)
    terms = lax.all_to_all(block, ("lon", "lat"), 0, 0, tiled=True)
    total = jnp.sum(terms.astype(F32), axis=0).astype(BF16)
    total = jnp.broadcast_to(total[None], terms.shape)
    return lax.all_to_all(total, ("lon", "lat"), 0, 0, tiled=True).reshape(count * chunk, 128)


def finish_kernel(fine_scale, coarse_scale, sums, project1, combine1, merge, project2, combine2):
    thin, width = combine1.shape[0], combine2.shape[0]
    at = 0

    def take(rows):
        nonlocal at
        at += rows
        return sums[at - rows : at, :].astype(F32)

    for j in range(width // 128):
        merge[:, j * 128 : (j + 1) * 128] = take(merge.shape[0]) * coarse_scale
    for i in range(3):
        for j in range(width // 128):
            lane = i * width + j * 128
            project2[:, lane : lane + 128] = take(width) * coarse_scale
    for j in range(width // 128):
        combine2[:, j * 128 : (j + 1) * 128] = take(width) * coarse_scale
    fine = jnp.concatenate([take(thin) for _ in range(4 * thin // 128)], axis=1) * fine_scale
    project1[...] = fine[:, : 3 * thin]
    combine1[...] = fine[:, 3 * thin :]


def local(
    fine_tokens, cotangent, fine_gain, fine_project, fine_combine, fine_table, fine_types,
    merge_gain, merge_weight, coarse_gain, coarse_project, coarse_combine, coarse_table,
    coarse_types, surface_type, latitude_valid, bias_index,
):
    _, rows1, cols1, d1 = fine_tokens.shape
    _, rows2, cols2, d2 = cotangent.shape
    n1, n2 = rows1 * cols1, rows2 * cols2
    h1, h2 = d1 // HEAD, d2 // HEAD
    lons, lats = lax.axis_size("lon"), lax.axis_size("lat")
    enter = Shift(rows1, cols1, 3, 6, raster(cols1), windowed(cols1), True)
    middle = Shift(rows1, cols1, 3, 6, windowed(cols1), merging(cols1), True)
    return_middle = Shift(rows1, cols1, 3, 6, merging(cols1), windowed(cols1), False)
    leave = Shift(rows1, cols1, 3, 6, windowed(cols1), raster(cols1), False)
    centre = Shift(rows2, cols2, 3, 6, raster(cols2), windowed(cols2), True)
    cleave = Shift(rows2, cols2, 3, 6, windowed(cols2), raster(cols2), False)
    fine_halo = [((2, s, d1), BF16) for s in enter.sizes]
    coarse_halo = [((2, s, d2), BF16) for s in centre.sizes]
    tokens = fine_tokens.reshape(2 * n1, d1)
    cot = cotangent.reshape(2 * n2, d2)

    halos = call(
        prepare_kernel, "prepare", fine_halo + coarse_halo, [],
        [enter.send, centre.send, tokens, cot], flops=10**9,
    )
    token_halo = exchange(halos[:3], -1)
    cot_halo = exchange(halos[3:], -1)

    place = jnp.stack([lax.axis_index("lat"), lax.axis_index("lon"), jnp.int32(lats)]).astype(jnp.int32)
    pairs = jnp.concatenate([bias_index[:72, :72].T, bias_index[72:, 72:].T], axis=0)
    pairs = jnp.pad(pairs, ((0, 0), (0, 56)))[:, None]

    def level_bias(name, where, table, types, level_rows, rows, cols):
        lists = jnp.swapaxes(table[0], 1, 2).reshape(-1, table.shape[2])
        lists = jnp.pad(lists, ((0, 0), (0, -lists.shape[1] % 128)))
        t = types.T
        t = jnp.pad(jnp.concatenate([t, t, t], axis=1), ((0, 0), (0, 128 - 9)))
        order = windowed(cols)
        r, c = np.zeros((rows * cols, 1), np.int32), np.zeros((rows * cols, 1), np.int32)
        for a in range(rows):
            for b in range(cols):
                r[order(a, b), 0], c[order(a, b), 0] = a + 3, b + 6
        heads = types.shape[1]
        count = pad8(lists.shape[0])
        return call(
            partial(bias_kernel, level_rows), name,
            [((2, rows // 6, 72, 72 * heads), F32), ((rows * cols, 128), F32), ((72 * heads, 128), BF16)],
            [((count * 144, 128), F32), ((count * lists.shape[1] // 128, 256), BF16)],
            [where, latitude_valid, pairs, lists, surface_type, t, r, c],
            smem=2, flops=4 * 10**9,
        )

    fbias, fkinds, ftyped = level_bias("fine_bias", place, fine_table, fine_types, 1, rows1, cols1)

    token16 = lambda width: ((2 * n1, width), BF16)
    blocks1 = 2 * n1 // 72
    forward = call(
        fine_forward_kernel, "fine_forward",
        [token16(d1)] + fine_halo + [token16(d1), ((blocks1, 72, 72 * h1), BF16), token16(d1)],
        [((2 * n1, d1), F32)] * 4,
        [enter.take, middle.send, tokens, *token_halo, fine_gain[None], fine_project, fine_combine,
         fbias, fkinds, ftyped],
        flops=4 * 10**9,
    )
    fine_output, kept = forward[0], forward[4:]
    halo = exchange(forward[1:4], -1)
    later, _ = lax.optimization_barrier((place, forward[1]))
    cbias, ckinds, ctyped = level_bias("coarse_bias", later, coarse_table, coarse_types, 2, rows2, cols2)

    rows = (4 * d1 + 4 * d2) * d2 // 128
    coarse = call(
        coarse_kernel, "coarse",
        [((2 * n2, d2), BF16)] + coarse_halo + [token16(d1)] + fine_halo + [((rows, 128), BF16)],
        [((2 * n2, d2), F32)] * 8 + [((8, 128), F32)],
        [middle.take, centre.take, cleave.send, return_middle.send, fine_output, *halo, cot, *cot_halo,
         merge_gain.reshape(4, d1), merge_weight, coarse_gain[None], coarse_project, coarse_combine,
         cbias, ckinds, ctyped],
        flops=6 * 10**9,
    )
    delta_halo = exchange(coarse[5:8], 1)
    out_halo = exchange(coarse[1:4], 1)

    backward = call(
        fine_backward_kernel, "fine_backward",
        [token16(d1)] + fine_halo + [((4 * d1 * d1 // 128, 128), BF16)],
        [((2 * n1, d1), F32)] * 7,
        [return_middle.take, leave.send, coarse[4], *delta_halo, *kept,
         fine_gain[None], fine_project, fine_combine],
        flops=6 * 10**9,
    )
    last_halo = exchange(backward[1:4], 1)

    (coarse_out,) = call(
        restore_kernel, "restore_coarse", [((2 * n2, d2), BF16)], [],
        [cleave.take, coarse[0], *out_halo],
    )
    (gradient,) = call(
        restore_kernel, "restore_fine", [token16(d1)], [],
        [leave.take, backward[0], *last_halo],
    )

    count = 2 * n1 * lons * lats
    fine_scale, coarse_scale = 1.0 / math.sqrt(count), 1.0 / math.sqrt(count // 4)
    sums = summed([coarse[8], backward[4]])
    gradients = call(
        partial(finish_kernel, fine_scale, coarse_scale), "finish",
        [((d1, 3 * d1), F32), ((d1, d1), F32), ((4 * d1, d2), F32), ((d2, 3 * d2), F32), ((d2, d2), F32)],
        [], [sums],
    )
    return (coarse_out.reshape(cotangent.shape), gradient.reshape(fine_tokens.shape), *gradients)


def solution(mesh):
    split = P(None, "lat", "lon", None)
    table = P(None, "lat", None, None)
    in_specs = (
        split, split, P(), P(), P(), table, P(), P(), P(), P(), P(), P(), table, P(), P(), P(), P(),
    )
    out_specs = (split, split, P(), P(), P(), P(), P())
    return jax.shard_map(local, mesh=mesh, in_specs=in_specs, out_specs=out_specs, check_vma=False)
```

```python
import math
from functools import partial

import numpy as np
import jax
import jax.numpy as jnp
from jax import lax
from jax.experimental import pallas as pl
from jax.experimental.pallas import tpu as pltpu
from jax.sharding import PartitionSpec as P

F32 = jnp.float32
BF16 = jnp.bfloat16
EPSILON = 1e-05
HEAD = 32
SCALE = HEAD ** (-0.5)
BLOCKED = -1e30
UNROLL = 4
NT = (((1,), (1,)), ((), ()))
TN = (((0,), (0,)), ((), ()))
NN = (((1,), (0,)), ((), ()))


def pad16(n):
    return (n + 15) // 16 * 16


class Shift:
    def __init__(self, rows, cols, dr, dc, source, target, forward):
        if forward:
            ranges = (
                (range(0, dr), range(dc, cols)),
                (range(dr, rows), range(0, dc)),
                (range(0, dr), range(0, dc)),
            )
        else:
            ranges = (
                (range(rows - dr, rows), range(0, cols - dc)),
                (range(0, rows - dr), range(cols - dc, cols)),
                (range(rows - dr, rows), range(cols - dc, cols)),
            )
        lists = [[(r, c) for r in rr for c in cc] for rr, cc in ranges]
        self.sizes = [pad16(len(x)) for x in lists]
        self.own = rows * cols
        send = []
        for x, size in zip(lists, self.sizes):
            send += [source(r, c) for r, c in x] + [0] * (size - len(x))
        self.send = np.array(send, np.int32)[:, None]
        offsets = [self.own, self.own + self.sizes[0], self.own + self.sizes[0] + self.sizes[1]]
        places = [{rc: o + n for n, rc in enumerate(x)} for x, o in zip(lists, offsets)]
        take = np.zeros((self.own, 1), np.int32)
        sign = 1 if forward else -1
        for r in range(rows):
            for c in range(cols):
                a, b = r + sign * dr, c + sign * dc
                out_row, out_col = not 0 <= a < rows, not 0 <= b < cols
                a, b = a % rows, b % cols
                if out_row or out_col:
                    which = 2 if out_row and out_col else (0 if out_row else 1)
                    place = places[which][(a, b)]
                else:
                    place = source(a, b)
                take[target(r, c), 0] = place
        self.take = take
        self.total = self.own + sum(self.sizes)


def pad8(n):
    return (n + 7) // 8 * 8


def raster(cols):
    return lambda r, c: r * cols + c


def windowed(cols):
    per_row = cols // 12
    return lambda r, c: ((r // 6) * per_row + c // 12) * 72 + (r % 6) * 12 + c % 12


def merging(cols):
    coarse = windowed(cols // 2)
    quarter = lambda rows: rows
    return lambda r, c: ((r % 2) * 2 + c % 2) * 144 + coarse(r // 2, c // 2)


def one_hot(index, width):
    lanes = lax.broadcasted_iota(jnp.int32, (index.shape[0], width), 1)
    return jnp.where(lanes == index, 1.0, 0.0).astype(BF16)


def mm(a, b, dims=NN):
    return lax.dot_general(a, b, dims, preferred_element_type=F32)


def round16(x):
    return x.astype(BF16).astype(F32)


def pick(take, total, own, parts):
    return mm(one_hot(take, total), jnp.concatenate([own] + parts, axis=0))


def head_masks(channels):
    lanes = lax.broadcasted_iota(jnp.int32, (1, channels), 1)
    return [
        jnp.where((lanes >= HEAD * h) & (lanes < HEAD * (h + 1)), 1.0, 0.0)
        for h in range(channels // HEAD)
    ]


def spread_heads(x, masks):
    return jnp.concatenate([x * m for m in masks], axis=0).astype(BF16)


def fold_heads(x, masks):
    out = x[0:72] * masks[0]
    for h in range(1, len(masks)):
        out = out + x[72 * h : 72 * (h + 1)] * masks[h]
    return out


def weights_of(k16, qbig, kinds16, types16, bias):
    x = mm(k16, qbig, NT) * SCALE + (mm(kinds16, types16) + bias)
    e = jnp.exp(x - jnp.max(x, axis=0, keepdims=True))
    return (e * (1.0 / jnp.sum(e, axis=0, keepdims=True))).astype(BF16)


def attention_back(q, k, v, p16, do, masks):
    k16 = k.astype(BF16)
    dobig = spread_heads(do, masks)
    qbig = spread_heads(q, masks)
    p = p16.astype(F32)
    dv = mm(p16, dobig)
    dp = round16(mm(v.astype(BF16), dobig, NT))
    pd = p * dp
    ds = ((pd - p * jnp.sum(pd, axis=0, keepdims=True)) * SCALE).astype(BF16)
    dq = fold_heads(mm(ds, k16, TN), masks)
    dk = mm(ds, qbig)
    return dq, dk, dv


def moments(parts):
    count = sum(x.shape[-1] for x in parts)
    mean = sum(jnp.sum(x, axis=-1, keepdims=True) for x in parts) * (1.0 / count)
    centred = [x - mean for x in parts]
    spread = sum(jnp.sum(c * c, axis=-1, keepdims=True) for c in centred) * (1.0 / count)
    return centred, lax.rsqrt(spread + EPSILON)


def norm_back(unit, inverse, gains, deltas):
    count = sum(x.shape[-1] for x in unit)
    scaled = [d * g for d, g in zip(deltas, gains)]
    mean = sum(jnp.sum(s, axis=-1, keepdims=True) for s in scaled) * (1.0 / count)
    along = sum(jnp.sum(s * u, axis=-1, keepdims=True) for s, u in zip(scaled, unit)) * (1.0 / count)
    return [(s - mean - u * along) * inverse for s, u in zip(scaled, unit)]


def send_out(index, own, refs, level):
    rows = mm(one_hot(index, own.shape[0]), own).astype(BF16)
    at = 0
    for ref in refs:
        n = ref.shape[1]
        ref[level] = rows[at : at + n]
        at += n


def prepare_kernel(fsel, csel, tokens, cot, fa, fb, fc, ca, cb, cc, fsel_s, csel_s, tokens_s, cot_s, sems):
    copies = [
        pltpu.make_async_copy(src, dst, sems.at[i])
        for i, (src, dst) in enumerate(((fsel, fsel_s), (tokens, tokens_s), (csel, csel_s), (cot, cot_s)))
    ]
    for copy in copies:
        copy.start()
    nf, nc = tokens.shape[0] // 2, cot.shape[0] // 2
    copies[0].wait()
    copies[1].wait()
    for level in range(2):
        send_out(fsel_s[...], tokens_s[level * nf : (level + 1) * nf, :], (fa, fb, fc), level)
    copies[2].wait()
    copies[3].wait()
    for level in range(2):
        send_out(csel_s[...], cot_s[level * nc : (level + 1) * nc, :], (ca, cb, cc), level)


def bias_kernel(
    level_rows, place, valid, index, table, surface, types, row, col,
    bias, kinds, typed, raw, parts,
):
    lat, lon, lats = place[0], place[1], place[2]
    windows, heads = bias.shape[1], bias.shape[3] // 72
    entries = table.shape[2]
    chunks = -(-entries // 128)
    count = windows * heads
    eights, half = count // 8, chunks // 2
    pieces = []
    for c in range(chunks):
        lanes = slice(c * 128, min(c * 128 + 128, entries))
        rows = [table[h, rw : rw + 1, lanes] for rw in range(windows) for h in range(heads)]
        piece = jnp.concatenate(rows, axis=0)
        if piece.shape[1] < 128:
            piece = jnp.concatenate([piece, jnp.zeros((count, 128 - piece.shape[1]), F32)], axis=1)
        pieces.append(piece)
    groups = [p[8 * g : 8 * g + 8] for g in range(eights) for p in pieces]
    if count % 8:
        groups += [jnp.concatenate([pieces[c][8 * eights :], pieces[c + half][8 * eights :]], axis=0) for c in range(half)]
    whole = jnp.concatenate(groups, axis=0)
    parts[:, 0:128] = whole.astype(BF16)
    parts[:, 128:256] = (whole - round16(whole)).astype(BF16)
    lanes_down = lax.broadcasted_iota(jnp.int32, (128, 256), 0)
    lower = jnp.where(lax.broadcasted_iota(jnp.int32, (8, 256), 0) >= 4, half, 0)

    def three_rows(i, carry):
        place = index[i]
        hot = jnp.where(lanes_down == (place & 127), 1.0, 0.0).astype(BF16)
        found = mm(parts[...], jnp.concatenate([hot, hot], axis=0))
        chunk = jnp.broadcast_to(place >> 7, (8, 256))

        def chosen(at, steps, chunk):
            total = jnp.zeros((8, 256), F32)
            for c in range(steps):
                total = jnp.where(chunk == c, found[at + 8 * c : at + 8 * c + 8, :], total)
            return total

        totals = [chosen(8 * chunks * g, chunks, chunk) for g in range(eights)]
        if count % 8:
            total = chosen(8 * chunks * eights, half, chunk - lower)
            totals.append(total + jnp.concatenate([total[4:], total[:4]], axis=0))
        for g, total in enumerate(totals):
            for r in range(3):
                row = jnp.concatenate([total[:, 72 * r : 72 * r + 72], jnp.zeros((8, 56), F32)], axis=1)
                raw[pl.ds(g * 1152 + 3 * i + r, 8, stride=144), :] = row
        return carry

    lax.fori_loop(0, 48, three_rows, 0, unroll=4)

    key = lax.broadcasted_iota(jnp.int32, (72, 72), 0)
    query = lax.broadcasted_iota(jnp.int32, (72, 72), 1)
    key_row = sum(jnp.where(key >= 12 * r, 1, 0) for r in range(1, 6))
    apart = jnp.where((key >= 36) != (query >= 36), 1, 0)
    rows, columns = surface.shape[0] // level_rows, surface.shape[1] // level_rows
    at_end = jnp.where(lat == lats - 1, 1, 0)
    for rw in range(windows):
        real = jnp.zeros((72, 72), jnp.int32)
        for r in range(6):
            spot = lax.rem(lat * (6 * windows) + (6 * rw + r + 3), rows) * level_rows
            here = valid[spot]
            for more in range(1, level_rows):
                here = jnp.maximum(here, valid[spot + more])
            real = jnp.where(key_row == r, here, real)
        good = (real == 1) | (key == query)
        if rw == windows - 1:
            good = good & (apart * at_end == 0)
        for level in range(2):
            for h in range(heads):
                at = (rw * heads + h) * 144 + level * 72
                bias[level, rw, :, 72 * h : 72 * (h + 1)] = jnp.where(
                    good, raw[at : at + 72, :][:, :72], BLOCKED
                )

    codes = surface[...].astype(F32).astype(BF16)
    tokens = kinds.shape[0]
    line = row[...] + lat * (6 * windows)
    line = jnp.where(line >= rows, line - rows, line) * level_rows
    spot = col[...] + lon * (12 * (tokens // 72 // windows))
    spot = jnp.where(spot >= columns, spot - columns, spot) * level_rows
    lines = mm(one_hot(line, surface.shape[0]), codes)
    lanes = lax.broadcasted_iota(jnp.int32, lines.shape, 1)
    code = jnp.sum(jnp.where(lanes == spot, lines, 0.0), axis=1, keepdims=True).astype(jnp.int32)
    lanes = lax.broadcasted_iota(jnp.int32, (tokens, 128), 1)
    kinds[...] = jnp.where((lanes == code) | (lanes == code + 3) | (lanes == code + 6), 1.0, 0.0)

    t = types[...]
    high = round16(t)
    middle = round16(t - high)
    lanes = lax.broadcasted_iota(jnp.int32, t.shape, 1)
    split = jnp.where(lanes < 3, high, jnp.where(lanes < 6, middle, t - high - middle))
    typed[...] = jnp.concatenate(
        [jnp.broadcast_to(split[h : h + 1], (72, 128)) for h in range(heads)], axis=0
    ).T.astype(BF16)


def fine_forward_kernel(
    take, sel, tokens, ra, rb, rc, gain, project, combine, bias, kinds, types,
    output, sa, sb, sc, kept_x, kept_p, kept_o,
    q_s, k_s, v_s, o_s,
):
    n = take.shape[0]
    width = tokens.shape[1]
    total = n + ra.shape[1] + rb.shape[1] + rc.shape[1]
    hot = one_hot(take[...], total)
    rolled = []
    for level in range(2):
        o = 1 - level
        source = jnp.concatenate([tokens[o * n : (o + 1) * n, :], ra[o], rb[o], rc[o]], axis=0)
        rolled.append(mm(hot, source))
    x = jnp.concatenate(rolled, axis=0)
    kept_x[...] = x.astype(BF16)
    (centred,), inverse = moments([x])
    u = (centred * inverse * gain[...]).astype(BF16)
    for i, scratch in enumerate((q_s, k_s, v_s)):
        scratch[...] = round16(mm(u, project[:, i * width : (i + 1) * width]))
    masks = head_masks(width)
    windows = n // 72
    across = windows // bias.shape[1]
    types16 = types[...]

    def window(w, carry):
        kinds16 = kinds[pl.ds(pl.multiple_of(w * 72, 8), 72), :].astype(BF16)
        for level in range(2):
            b = level * windows + w
            rows = pl.ds(pl.multiple_of(b * 72, 8), 72)
            qbig = spread_heads(q_s[rows, :], masks)
            p = weights_of(k_s[rows, :].astype(BF16), qbig, kinds16, types16, bias[level, w // across])
            kept_p[b] = p
            o_s[rows, :] = fold_heads(mm(p, v_s[rows, :].astype(BF16), TN), masks)
        return carry

    lax.fori_loop(0, windows, window, 0, unroll=UNROLL)
    o16 = o_s[...].astype(BF16)
    kept_o[...] = o16
    out = (x + mm(o16, combine[...])).astype(BF16)
    output[...] = out
    for level in range(2):
        send_out(sel[...], out[level * n : (level + 1) * n], (sa, sb, sc), level)


def coarse_kernel(
    take, ctake, csel, fsel, fine, ra, rb, rc, cot, da, db, dc,
    merge_gain, merge_weight, gain, project, combine, bias, kinds, types,
    output, oa, ob, oc, delta_fine, sa, sb, sc, kept_merged, kept,
    q_s, k_s, v_s, o_s, do_s, dq_s, dk_s, dv_s,
):
    n = take.shape[0]
    quarter = n // 4
    thin = fine.shape[1]
    width = combine.shape[0]
    total = n + ra.shape[1] + rb.shape[1] + rc.shape[1]
    hot = one_hot(take[...], total)
    ctotal = quarter + da.shape[1] + db.shape[1] + dc.shape[1]
    chot = one_hot(ctake[...], ctotal)
    levels, cot_levels = [], []
    for level in range(2):
        source = jnp.concatenate([fine[level * n : (level + 1) * n, :], ra[level], rb[level], rc[level]], axis=0)
        levels.append(mm(hot, source))
        o = 1 - level
        source = jnp.concatenate([cot[o * quarter : (o + 1) * quarter, :], da[o], db[o], dc[o]], axis=0)
        cot_levels.append(mm(chot, source))
    cells = [
        jnp.concatenate([x[s * quarter : (s + 1) * quarter] for x in levels], axis=0) for s in range(4)
    ]
    d = jnp.concatenate(cot_levels, axis=0)
    d16 = d.astype(BF16)
    merge_gains = [merge_gain[s : s + 1, :] for s in range(4)]
    m_centred, m_inverse = moments(cells)
    merged = [(c * m_inverse * g).astype(BF16) for c, g in zip(m_centred, merge_gains)]
    weight = [merge_weight[s * thin : (s + 1) * thin, :] for s in range(4)]
    entered = sum(mm(a, w) for a, w in zip(merged, weight))
    x = round16(entered)
    (centred,), inverse = moments([x])
    u = (centred * inverse * gain[...]).astype(BF16)
    wq, wk, wv = (project[:, i * width : (i + 1) * width] for i in range(3))
    q_s[...] = round16(mm(u, wq))
    k_s[...] = round16(mm(u, wk))
    v_s[...] = round16(mm(u, wv))
    do_s[...] = round16(mm(d16, combine[...], NT))
    masks = head_masks(width)
    windows = quarter // 72
    types16 = types[...]

    def window(w, carry):
        kinds16 = kinds[pl.ds(pl.multiple_of(w * 72, 8), 72), :].astype(BF16)
        for level in range(2):
            rows = pl.ds(pl.multiple_of((level * windows + w) * 72, 8), 72)
            q, k, v = q_s[rows, :], k_s[rows, :], v_s[rows, :]
            p = weights_of(k.astype(BF16), spread_heads(q, masks), kinds16, types16, bias[level, 0])
            o_s[rows, :] = fold_heads(mm(p, v.astype(BF16), TN), masks)
            dq, dk, dv = attention_back(q, k, v, p, do_s[rows, :], masks)
            dq_s[rows, :] = dq
            dk_s[rows, :] = dk
            dv_s[rows, :] = dv
        return carry

    lax.fori_loop(0, windows, window, 0, unroll=2)
    o16 = o_s[...].astype(BF16)
    out = (x + mm(o16, combine[...])).astype(BF16)
    output[...] = out
    for level in range(2):
        send_out(csel[...], out[level * quarter : (level + 1) * quarter], (oa, ob, oc), level)
    dq16, dk16, dv16 = dq_s[...].astype(BF16), dk_s[...].astype(BF16), dv_s[...].astype(BF16)
    delta_rolled = round16(mm(dq16, wq, NT) + mm(dk16, wk, NT) + mm(dv16, wv, NT))
    (dx,) = norm_back([centred * inverse], inverse, [gain[...]], [delta_rolled])
    delta = (d + round16(dx)).astype(BF16)
    deltas = [round16(mm(delta, w, NT)) for w in weight]
    back = norm_back([c * m_inverse for c in m_centred], m_inverse, merge_gains, deltas)
    back = [b.astype(BF16) for b in back]
    for level in range(2):
        own = jnp.concatenate([b[level * quarter : (level + 1) * quarter] for b in back], axis=0)
        delta_fine[level * n : (level + 1) * n, :] = own
        send_out(fsel[...], own, (sa, sb, sc), level)
    for s in range(4):
        kept_merged[s] = merged[s]
    for i, x in enumerate((u, dq16, dk16, dv16, o16, d16, delta)):
        kept[i] = x


def coarse_gradient_kernel(merged, kept, gradients):
    u, dq16, dk16, dv16, o16, d16, delta = (kept[i] for i in range(7))
    sums = [jnp.concatenate([mm(merged[s], delta, TN) for s in range(4)], axis=0)]
    sums += [mm(left, right, TN) for left, right in ((u, dq16), (u, dk16), (u, dv16), (o16, d16))]
    at = 0
    for block in sums:
        for j in range(block.shape[1] // 128):
            gradients[at : at + block.shape[0], :] = block[:, j * 128 : (j + 1) * 128].astype(BF16)
            at += block.shape[0]


def fine_again_kernel(kept_x, gain, project, kept_u, unit, inverse_out, q, k, v):
    width = kept_x.shape[1]
    (centred,), inverse = moments([kept_x[...].astype(F32)])
    scaled = centred * inverse
    u = (scaled * gain[...]).astype(BF16)
    kept_u[...] = u
    unit[...] = scaled
    inverse_out[...] = jnp.broadcast_to(inverse, inverse_out.shape)
    for i, out in enumerate((q, k, v)):
        out[...] = round16(mm(u, project[:, i * width : (i + 1) * width]))


def fine_backward_kernel(
    take, sel, own, ra, rb, rc, unit, inverse, q_s, k_s, v_s, kept_p, gain, project, combine,
    output, sa, sb, sc, kept,
    do_s, dq_s, dk_s, dv_s,
):
    n = take.shape[0]
    width = unit.shape[1]
    total = n + ra.shape[1] + rb.shape[1] + rc.shape[1]
    hot = one_hot(take[...], total)
    d = jnp.concatenate(
        [
            mm(hot, jnp.concatenate([own[l * n : (l + 1) * n, :], ra[l], rb[l], rc[l]], axis=0))
            for l in range(2)
        ],
        axis=0,
    )
    d16 = d.astype(BF16)
    do_s[...] = round16(mm(d16, combine[...], NT))
    masks = head_masks(width)
    windows = n // 72

    def window(w, carry):
        for level in range(2):
            b = level * windows + w
            rows = pl.ds(pl.multiple_of(b * 72, 8), 72)
            dq, dk, dv = attention_back(
                q_s[rows, :], k_s[rows, :], v_s[rows, :], kept_p[b], do_s[rows, :], masks
            )
            dq_s[rows, :] = dq
            dk_s[rows, :] = dk
            dv_s[rows, :] = dv
        return carry

    lax.fori_loop(0, windows, window, 0, unroll=UNROLL)
    parts = [dq_s[...].astype(BF16), dk_s[...].astype(BF16), dv_s[...].astype(BF16)]
    delta_rolled = round16(
        sum(mm(a, project[:, i * width : (i + 1) * width], NT) for i, a in enumerate(parts))
    )
    (dx,) = norm_back([unit[...]], inverse[:, 0:1], [gain[...]], [delta_rolled])
    out = (d + round16(dx)).astype(BF16)
    output[...] = out
    for level in range(2):
        send_out(sel[...], out[level * n : (level + 1) * n], (sa, sb, sc), level)
    for i, x in enumerate(parts + [d16]):
        kept[i] = x


def fine_gradient_kernel(kept_u, kept_o, kept, coarse, gradients):
    width, at = kept_u.shape[1], coarse.shape[0]
    gradients[:at, :] = coarse[...]
    pieces = [mm(kept_u[...], kept[i], TN) for i in range(3)] + [mm(kept_o[...], kept[3], TN)]
    pieces = jnp.concatenate(pieces, axis=1).astype(BF16)
    for j in range(pieces.shape[1] // 128):
        gradients[at : at + width, :] = pieces[:, j * 128 : (j + 1) * 128]
        at += width
    gradients[at:, :] = jnp.zeros((gradients.shape[0] - at, 128), BF16)


def restore_kernel(take, own, ra, rb, rc, output):
    n = take.shape[0]
    hot = one_hot(take[...], n + ra.shape[1] + rb.shape[1] + rc.shape[1])
    for level in range(2):
        o = 1 - level
        source = jnp.concatenate([own[o * n : (o + 1) * n, :], ra[o], rb[o], rc[o]], axis=0)
        output[level * n : (level + 1) * n, :] = mm(hot, source).astype(BF16)


VMEM = pl.BlockSpec(memory_space=pltpu.VMEM)
SMEM = pl.BlockSpec(memory_space=pltpu.SMEM)


LIMITS = {"fine_bias": 6, "coarse_bias": 6, "fine_again": 8, "coarse_gradients": 6, "fine_gradients": 6, "restore_coarse": 4, "restore_fine": 6, "add": 4, "finish": 6}


def call(kernel, name, outs, scratch, args, smem=0, flops=10**9, limit=16, space=pltpu.VMEM, copies=0):
    limit = LIMITS.get(name, limit)
    given = pl.BlockSpec(memory_space=space)
    semaphores = [pltpu.SemaphoreType.DMA((copies,))] if copies else []
    return pl.pallas_call(
        kernel,
        name=name,
        out_shape=[jax.ShapeDtypeStruct(s, d) for s, d in outs],
        in_specs=[SMEM] * smem + [given] * (len(args) - smem),
        out_specs=[VMEM] * len(outs),
        scratch_shapes=[pltpu.VMEM(s, d) for s, d in scratch] + semaphores,
        cost_estimate=pl.CostEstimate(flops=flops, bytes_accessed=4 << 20, transcendentals=0),
        compiler_params=pltpu.CompilerParams(vmem_limit_bytes=limit << 20),
    )(*args)


def move(value, lat_step, lon_step):
    lons, lats = lax.axis_size("lon"), lax.axis_size("lat")
    if lat_step == 0:
        return lax.ppermute(value, "lon", [(s, (s + lon_step) % lons) for s in range(lons)])
    if lon_step == 0:
        return lax.ppermute(value, "lat", [(s, (s + lat_step) % lats) for s in range(lats)])
    pairs = [
        (a * lats + b, ((a + lon_step) % lons) * lats + (b + lat_step) % lats)
        for a in range(lons)
        for b in range(lats)
    ]
    return lax.ppermute(value, ("lon", "lat"), pairs)


def exchange(parts, step):
    a, b, c = parts
    return [move(a, step, 0), move(b, 0, step), move(c, step, step)]


def add_kernel(terms, repeated):
    count = terms.shape[0]

    def eight(i, total):
        return total + sum(terms[8 * i + j].astype(F32) for j in range(8))

    total = lax.fori_loop(0, count // 8, eight, jnp.zeros(terms.shape[1:], F32)).astype(BF16)

    def store(i, carry):
        for j in range(8):
            repeated[8 * i + j] = total
        return carry

    lax.fori_loop(0, count // 8, store, 0)


def summed(block, before):
    count = lax.axis_size("lon") * lax.axis_size("lat")
    block = block.reshape(count, -1, 128)
    terms = lax.all_to_all(block, ("lon", "lat"), 0, 0, tiled=True)
    terms, *before = lax.optimization_barrier((terms, *before))
    (total,) = call(add_kernel, "add", [(block.shape, BF16)], [], [terms])
    return lax.all_to_all(total, ("lon", "lat"), 0, 0, tiled=True).reshape(-1, 128), before


def finish_kernel(fine_scale, coarse_scale, sums, project1, combine1, merge, project2, combine2):
    thin, width = combine1.shape[0], combine2.shape[0]
    at = 0
    for block, lanes in ((merge, range(1)), (project2, range(3)), (combine2, range(1))):
        for i in lanes:
            for j in range(width // 128):
                rows, lane = block.shape[0], i * width + j * 128
                block[:, lane : lane + 128] = sums[at : at + rows, :].astype(F32) * coarse_scale
                at += rows
    pieces = [sums[at + j * thin : at + (j + 1) * thin, :].astype(F32) for j in range(4 * thin // 128)]
    whole = jnp.concatenate(pieces, axis=1) * fine_scale
    project1[...] = whole[:, : 3 * thin]
    combine1[...] = whole[:, 3 * thin :]


def local(
    fine_tokens, cotangent, fine_gain, fine_project, fine_combine, fine_table, fine_types,
    merge_gain, merge_weight, coarse_gain, coarse_project, coarse_combine, coarse_table,
    coarse_types, surface_type, latitude_valid, bias_index,
):
    _, rows1, cols1, d1 = fine_tokens.shape
    _, rows2, cols2, d2 = cotangent.shape
    n1, n2 = rows1 * cols1, rows2 * cols2
    h1, h2 = d1 // HEAD, d2 // HEAD
    lons, lats = lax.axis_size("lon"), lax.axis_size("lat")
    enter = Shift(rows1, cols1, 3, 6, raster(cols1), windowed(cols1), True)
    middle = Shift(rows1, cols1, 3, 6, windowed(cols1), merging(cols1), True)
    return_middle = Shift(rows1, cols1, 3, 6, merging(cols1), windowed(cols1), False)
    leave = Shift(rows1, cols1, 3, 6, windowed(cols1), raster(cols1), False)
    centre = Shift(rows2, cols2, 3, 6, raster(cols2), windowed(cols2), True)
    cleave = Shift(rows2, cols2, 3, 6, windowed(cols2), raster(cols2), False)
    fine_halo = [((2, s, d1), BF16) for s in enter.sizes]
    coarse_halo = [((2, s, d2), BF16) for s in centre.sizes]
    tokens = fine_tokens.reshape(2 * n1, d1)
    cot = cotangent.reshape(2 * n2, d2)

    halos = call(
        prepare_kernel, "prepare", fine_halo + coarse_halo,
        [(x.shape, x.dtype) for x in (enter.send, centre.send, tokens, cot)],
        [enter.send, centre.send, tokens, cot], limit=60, space=pltpu.HBM, copies=4,
    )
    token_halo = exchange(halos[:3], -1)
    cot_halo = exchange(halos[3:], -1)

    place = jnp.stack([lax.axis_index("lat"), lax.axis_index("lon"), jnp.int32(lats)]).astype(jnp.int32)
    pairs = jnp.concatenate([bias_index[:72, :72].T, bias_index[72:, 72:].T], axis=0)
    pairs = jnp.pad(pairs.reshape(48, 216), ((0, 0), (0, 40)))[:, None]

    def level_bias(name, where, table, types, level_rows, rows, cols):
        lists = jnp.transpose(table[0], (2, 0, 1))
        t = types.T
        t = jnp.pad(jnp.concatenate([t, t, t], axis=1), ((0, 0), (0, 128 - 9)))
        order = windowed(cols)
        r, c = np.zeros((rows * cols, 1), np.int32), np.zeros((rows * cols, 1), np.int32)
        for a in range(rows):
            for b in range(cols):
                r[order(a, b), 0], c[order(a, b), 0] = a + 3, b + 6
        heads = types.shape[1]
        count = lists.shape[0] * lists.shape[1]
        chunks = -(-lists.shape[2] // 128)
        return call(
            partial(bias_kernel, level_rows), name,
            [((2, rows // 6, 72, 72 * heads), F32), ((rows * cols, 128), F32), ((128, 72 * heads), BF16)],
            [((pad8(count) * 144, 128), F32), ((count * chunks, 256), BF16)],
            [where, latitude_valid, pairs, lists, surface_type, t, r, c],
            smem=2, flops=4 * 10**9,
        )

    fbias, fkinds, ftyped = level_bias("fine_bias", place, fine_table, fine_types, 1, rows1, cols1)

    token16 = lambda width: ((2 * n1, width), BF16)
    blocks1 = 2 * n1 // 72
    forward = call(
        fine_forward_kernel, "fine_forward",
        [token16(d1)] + fine_halo + [token16(d1), ((blocks1, 72, 72 * h1), BF16), token16(d1)],
        [((2 * n1, d1), F32)] * 4,
        [enter.take, middle.send, tokens, *token_halo, fine_gain[None], fine_project, fine_combine,
         fbias, fkinds, ftyped],
        flops=4 * 10**9,
    )
    fine_output, kept = forward[0], forward[4:]
    halo = exchange(forward[1:4], -1)
    later, _ = lax.optimization_barrier((place, forward[1]))
    cbias, ckinds, ctyped = level_bias("coarse_bias", later, coarse_table, coarse_types, 2, rows2, cols2)

    rows = (4 * d1 + 4 * d2) * d2 // 128
    coarse = call(
        coarse_kernel, "coarse",
        [((2 * n2, d2), BF16)] + coarse_halo + [token16(d1)] + fine_halo
        + [((4, 2 * n2, d1), BF16), ((7, 2 * n2, d2), BF16)],
        [((2 * n2, d2), F32)] * 8,
        [middle.take, centre.take, cleave.send, return_middle.send, fine_output, *halo, cot, *cot_halo,
         merge_gain.reshape(4, d1), merge_weight, coarse_gain[None], coarse_project, coarse_combine,
         cbias, ckinds, ctyped],
        flops=6 * 10**9,
    )
    delta_halo = exchange(coarse[5:8], 1)
    out_halo = exchange(coarse[1:4], 1)
    kept_x, kept_p, kept_o, after = lax.optimization_barrier((*kept, coarse[8]))
    (coarse_sums,) = call(
        coarse_gradient_kernel, "coarse_gradients", [((rows, 128), BF16)], [], [after, coarse[9]], flops=2 * 10**9,
    )
    wide = ((2 * n1, d1), F32)
    u, unit, inverse, q, k, v = call(
        fine_again_kernel, "fine_again", [token16(d1), wide, ((2 * n1, 128), F32), wide, wide, wide], [],
        [kept_x, fine_gain[None], fine_project], flops=2 * 10**9,
    )
    backward = call(
        fine_backward_kernel, "fine_backward",
        [token16(d1)] + fine_halo + [((4, 2 * n1, d1), BF16)],
        [wide] * 4,
        [return_middle.take, leave.send, coarse[4], *delta_halo, unit, inverse, q, k, v, kept_p,
         fine_gain[None], fine_project, fine_combine],
        flops=6 * 10**9,
    )
    last_halo = exchange(backward[1:4], 1)
    count = lons * lats
    chunk = pad16(-(-(rows + 4 * d1 * d1 // 128) // count))
    (sums,) = call(
        fine_gradient_kernel, "fine_gradients", [((count * chunk, 128), BF16)], [],
        [u, kept_o, backward[4], coarse_sums], flops=2 * 10**9,
    )
    sums, *out_halo = lax.optimization_barrier((sums, *out_halo))
    sums, last_halo = summed(sums, last_halo)

    (coarse_out,) = call(
        restore_kernel, "restore_coarse", [((2 * n2, d2), BF16)], [],
        [cleave.take, coarse[0], *out_halo],
    )
    count = 2 * n1 * lons * lats
    fine_scale, coarse_scale = 1.0 / math.sqrt(count), 1.0 / math.sqrt(count // 4)
    (gradient,) = call(
        restore_kernel, "restore_fine", [token16(d1)], [],
        [leave.take, backward[0], *last_halo],
    )
    gradients = call(
        partial(finish_kernel, fine_scale, coarse_scale), "finish",
        [((d1, 3 * d1), F32), ((d1, d1), F32), ((4 * d1, d2), F32), ((d2, 3 * d2), F32), ((d2, d2), F32)],
        [], [sums],
    )
    return (coarse_out.reshape(cotangent.shape), gradient.reshape(fine_tokens.shape), *gradients)


def solution(mesh):
    split = P(None, "lat", "lon", None)
    table = P(None, "lat", None, None)
    in_specs = (
        split, split, P(), P(), P(), table, P(), P(), P(), P(), P(), P(), table, P(), P(), P(), P(),
    )
    out_specs = (split, split, P(), P(), P(), P(), P())
    return jax.shard_map(local, mesh=mesh, in_specs=in_specs, out_specs=out_specs, check_vma=False)
```

```python
import math
from functools import partial

import numpy as np
import jax
import jax.numpy as jnp
from jax import lax
from jax.experimental import pallas as pl
from jax.experimental.pallas import tpu as pltpu
from jax.sharding import PartitionSpec as P

F32 = jnp.float32
BF16 = jnp.bfloat16
EPSILON = 1e-05
HEAD = 32
SCALE = HEAD ** (-0.5)
BLOCKED = -1e30
UNROLL = 2
TOGETHER = 2
NT = (((1,), (1,)), ((), ()))
TN = (((0,), (0,)), ((), ()))
NN = (((1,), (0,)), ((), ()))


def pad16(n):
    return (n + 15) // 16 * 16


class Shift:
    def __init__(self, rows, cols, dr, dc, source, target, forward):
        if forward:
            ranges = (
                (range(0, dr), range(dc, cols)),
                (range(dr, rows), range(0, dc)),
                (range(0, dr), range(0, dc)),
            )
        else:
            ranges = (
                (range(rows - dr, rows), range(0, cols - dc)),
                (range(0, rows - dr), range(cols - dc, cols)),
                (range(rows - dr, rows), range(cols - dc, cols)),
            )
        lists = [[(r, c) for r in rr for c in cc] for rr, cc in ranges]
        self.sizes = [pad16(len(x)) for x in lists]
        self.own = rows * cols
        send = []
        for x, size in zip(lists, self.sizes):
            send += [source(r, c) for r, c in x] + [0] * (size - len(x))
        self.send = np.array(send, np.int32)[:, None]
        offsets = [self.own, self.own + self.sizes[0], self.own + self.sizes[0] + self.sizes[1]]
        places = [{rc: o + n for n, rc in enumerate(x)} for x, o in zip(lists, offsets)]
        take = np.zeros((self.own, 1), np.int32)
        sign = 1 if forward else -1
        for r in range(rows):
            for c in range(cols):
                a, b = r + sign * dr, c + sign * dc
                out_row, out_col = not 0 <= a < rows, not 0 <= b < cols
                a, b = a % rows, b % cols
                if out_row or out_col:
                    which = 2 if out_row and out_col else (0 if out_row else 1)
                    place = places[which][(a, b)]
                else:
                    place = source(a, b)
                take[target(r, c), 0] = place
        self.take = take
        self.total = self.own + sum(self.sizes)


def pad8(n):
    return (n + 7) // 8 * 8


def raster(cols):
    return lambda r, c: r * cols + c


def windowed(cols):
    per_row = cols // 12
    return lambda r, c: ((r // 6) * per_row + c // 12) * 72 + (r % 6) * 12 + c % 12


def merging(cols):
    coarse = windowed(cols // 2)
    quarter = lambda rows: rows
    return lambda r, c: ((r % 2) * 2 + c % 2) * 144 + coarse(r // 2, c // 2)


def one_hot(index, width):
    lanes = lax.broadcasted_iota(jnp.int32, (index.shape[0], width), 1)
    return jnp.where(lanes == index, 1.0, 0.0).astype(BF16)


def mm(a, b, dims=NN):
    return lax.dot_general(a, b, dims, preferred_element_type=F32)


def round16(x):
    return x.astype(BF16).astype(F32)


def pick(take, total, own, parts):
    return mm(one_hot(take, total), jnp.concatenate([own] + parts, axis=0))


def head_masks(channels):
    lanes = lax.broadcasted_iota(jnp.int32, (1, channels), 1)
    return [
        jnp.where((lanes >= HEAD * h) & (lanes < HEAD * (h + 1)), 1.0, 0.0)
        for h in range(channels // HEAD)
    ]


def lane_groups(channels):
    return [
        (slice(c, min(c + 128, channels)), slice(0, 72 * ((min(c + 128, channels) - c) // HEAD)))
        for c in range(0, channels, 128)
    ]


def spread_heads(x):
    return jnp.concatenate([x * m for m in head_masks(x.shape[1])], axis=0).astype(BF16)


def fold_heads(x):
    masks = head_masks(x.shape[1])
    out = x[0:72] * masks[0]
    for h in range(1, len(masks)):
        out = out + x[72 * h : 72 * (h + 1)] * masks[h]
    return out


def attention_forward(blocks, bias, scores):
    spread = [spread_heads(q) for q, _, _ in blocks]
    x = [mm(k.astype(BF16), s, NT) * SCALE for (_, k, _), s in zip(blocks, spread)]
    x = [a + (t + b) for a, t, b in zip(x, scores, bias)]
    e = [jnp.exp(a - jnp.max(a, axis=0, keepdims=True)) for a in x]
    p = [(a * (1.0 / jnp.sum(a, axis=0, keepdims=True))).astype(BF16) for a in e]
    mixed = [mm(a, v.astype(BF16), TN) for a, (_, _, v) in zip(p, blocks)]
    return p, [fold_heads(m) for m in mixed]


def attention_back(blocks, weights, deltas):
    spread = [spread_heads(d) for d in deltas]
    dp = [mm(v.astype(BF16), d, NT) for (_, _, v), d in zip(blocks, spread)]
    dv = [mm(p, d) for p, d in zip(weights, spread)]
    ds = []
    for p16, d in zip(weights, dp):
        p = p16.astype(F32)
        pd = p * round16(d)
        ds.append(((pd - p * jnp.sum(pd, axis=0, keepdims=True)) * SCALE).astype(BF16))
    dq = [mm(d, k.astype(BF16), TN) for d, (_, k, _) in zip(ds, blocks)]
    dk = [mm(d, spread_heads(q)) for d, (q, _, _) in zip(ds, blocks)]
    return [(fold_heads(x), y, z) for x, y, z in zip(dq, dk, dv)]


def window_rows(windows, first, count):
    return [
        (level, first + i, pl.ds(pl.multiple_of((level * windows + first + i) * 72, 8), 72))
        for i in range(count)
        for level in range(2)
    ]


def moments(parts):
    count = sum(x.shape[-1] for x in parts)
    mean = sum(jnp.sum(x, axis=-1, keepdims=True) for x in parts) * (1.0 / count)
    centred = [x - mean for x in parts]
    spread = sum(jnp.sum(c * c, axis=-1, keepdims=True) for c in centred) * (1.0 / count)
    return centred, lax.rsqrt(spread + EPSILON)


def norm_back(unit, inverse, gains, deltas):
    count = sum(x.shape[-1] for x in unit)
    scaled = [d * g for d, g in zip(deltas, gains)]
    mean = sum(jnp.sum(s, axis=-1, keepdims=True) for s in scaled) * (1.0 / count)
    along = sum(jnp.sum(s * u, axis=-1, keepdims=True) for s, u in zip(scaled, unit)) * (1.0 / count)
    return [(s - mean - u * along) * inverse for s, u in zip(scaled, unit)]


def send_out(index, own, refs, level):
    rows = mm(one_hot(index, own.shape[0]), own).astype(BF16)
    at = 0
    for ref in refs:
        n = ref.shape[1]
        ref[level] = rows[at : at + n]
        at += n


def prepare_kernel(fsel, csel, tokens, cot, fa, fb, fc, ca, cb, cc, fsel_s, csel_s, tokens_s, cot_s, sems):
    copies = [
        pltpu.make_async_copy(src, dst, sems.at[i])
        for i, (src, dst) in enumerate(((fsel, fsel_s), (tokens, tokens_s), (csel, csel_s), (cot, cot_s)))
    ]
    for copy in copies:
        copy.start()
    nf, nc = tokens.shape[0] // 2, cot.shape[0] // 2
    copies[0].wait()
    copies[1].wait()
    for level in range(2):
        send_out(fsel_s[...], tokens_s[level * nf : (level + 1) * nf, :], (fa, fb, fc), level)
    copies[2].wait()
    copies[3].wait()
    for level in range(2):
        send_out(csel_s[...], cot_s[level * nc : (level + 1) * nc, :], (ca, cb, cc), level)


def bias_kernel(
    level_rows, size, place, valid, index, table, bias, raw, parts,
):
    lat, lon, lats = place[0], place[1], place[2]
    windows, heads = bias.shape[1], table.shape[0]
    run = bias.shape[4] // 72
    entries = table.shape[2]
    chunks = -(-entries // 128)
    count = windows * heads
    eights, half = count // 8, chunks // 2
    pieces = []
    for c in range(chunks):
        lanes = slice(c * 128, min(c * 128 + 128, entries))
        rows = [table[h, rw : rw + 1, lanes] for rw in range(windows) for h in range(heads)]
        piece = jnp.concatenate(rows, axis=0)
        if piece.shape[1] < 128:
            piece = jnp.concatenate([piece, jnp.zeros((count, 128 - piece.shape[1]), F32)], axis=1)
        pieces.append(piece)
    groups = [p[8 * g : 8 * g + 8] for g in range(eights) for p in pieces]
    if count % 8:
        groups += [jnp.concatenate([pieces[c][8 * eights :], pieces[c + half][8 * eights :]], axis=0) for c in range(half)]
    whole = jnp.concatenate(groups, axis=0)
    parts[:, 0:128] = whole.astype(BF16)
    parts[:, 128:256] = (whole - round16(whole)).astype(BF16)
    lanes_down = lax.broadcasted_iota(jnp.int32, (128, 256), 0)
    lower = jnp.where(lax.broadcasted_iota(jnp.int32, (8, 256), 0) >= 4, half, 0)

    def three_rows(i, carry):
        place = index[i]
        hot = jnp.where(lanes_down == (place & 127), 1.0, 0.0).astype(BF16)
        found = mm(parts[...], jnp.concatenate([hot, hot], axis=0))
        chunk = jnp.broadcast_to(place >> 7, (8, 256))

        def chosen(at, steps, chunk):
            total = jnp.zeros((8, 256), F32)
            for c in range(steps):
                total = jnp.where(chunk == c, found[at + 8 * c : at + 8 * c + 8, :], total)
            return total

        totals = [chosen(8 * chunks * g, chunks, chunk) for g in range(eights)]
        if count % 8:
            total = chosen(8 * chunks * eights, half, chunk - lower)
            totals.append(total + jnp.concatenate([total[4:], total[:4]], axis=0))
        for g, total in enumerate(totals):
            for r in range(3):
                row = jnp.concatenate([total[:, 72 * r : 72 * r + 72], jnp.zeros((8, 56), F32)], axis=1)
                raw[pl.ds(g * 1152 + 3 * i + r, 8, stride=144), :] = row
        return carry

    lax.fori_loop(0, 48, three_rows, 0, unroll=4)

    key = lax.broadcasted_iota(jnp.int32, (72, 72), 0)
    query = lax.broadcasted_iota(jnp.int32, (72, 72), 1)
    key_row = sum(jnp.where(key >= 12 * r, 1, 0) for r in range(1, 6))
    apart = jnp.where((key >= 36) != (query >= 36), 1, 0)
    rows = size // level_rows
    at_end = jnp.where(lat == lats - 1, 1, 0)
    for rw in range(windows):
        real = jnp.zeros((72, 72), jnp.int32)
        for r in range(6):
            spot = lax.rem(lat * (6 * windows) + (6 * rw + r + 3), rows) * level_rows
            here = valid[spot]
            for more in range(1, level_rows):
                here = jnp.maximum(here, valid[spot + more])
            real = jnp.where(key_row == r, here, real)
        good = (real == 1) | (key == query)
        if rw == windows - 1:
            good = good & (apart * at_end == 0)
        for level in range(2):
            for h in range(heads):
                at = (rw * heads + h) * 144 + level * 72
                bias[level, rw, h // run, :, 72 * (h % run) : 72 * (h % run + 1)] = jnp.where(
                    good, raw[at : at + 72, :][:, :72], BLOCKED
                )


def kinds_of(lat, lon, windows, level_rows, surface, row, col):
    rows, columns = surface.shape[0] // level_rows, surface.shape[1] // level_rows
    codes = surface[...].astype(F32).astype(BF16)
    tokens = row.shape[0]
    line = row[...] + lat * (6 * windows)
    line = jnp.where(line >= rows, line - rows, line) * level_rows
    spot = col[...] + lon * (12 * (tokens // 72 // windows))
    spot = jnp.where(spot >= columns, spot - columns, spot) * level_rows
    lines = mm(one_hot(line, surface.shape[0]), codes)
    lanes = lax.broadcasted_iota(jnp.int32, lines.shape, 1)
    code = jnp.sum(jnp.where(lanes == spot, lines, 0.0), axis=1, keepdims=True).astype(jnp.int32)
    lanes = lax.broadcasted_iota(jnp.int32, (tokens, 128), 1)
    return jnp.where((lanes == code) | (lanes == code + 3) | (lanes == code + 6), 1.0, 0.0)


def types_of(types):
    t = types[...]
    high = round16(t)
    middle = round16(t - high)
    lanes = lax.broadcasted_iota(jnp.int32, t.shape, 1)
    split = jnp.where(lanes < 3, high, jnp.where(lanes < 6, middle, t - high - middle))
    rows = [jnp.broadcast_to(split[h : h + 1], (72, 128)) for h in range(t.shape[0])]
    return [jnp.concatenate(rows[h : h + 4], axis=0).T.astype(BF16) for h in range(0, len(rows), 4)]


def fine_forward_kernel(
    place, take, sel, tokens, ra, rb, rc, gain, project, combine, bias, surface, types, row, col,
    output, sa, sb, sc, kept_x, kept_p, kept_o,
    q_s, k_s, v_s, o_s, kinds,
):
    n = take.shape[0]
    width = tokens.shape[1]
    total = n + ra.shape[1] + rb.shape[1] + rc.shape[1]
    hot = one_hot(take[...], total)
    rolled = []
    for level in range(2):
        o = 1 - level
        source = jnp.concatenate([tokens[o * n : (o + 1) * n, :], ra[o], rb[o], rc[o]], axis=0)
        rolled.append(mm(hot, source))
    x = jnp.concatenate(rolled, axis=0)
    kept_x[...] = x.astype(BF16)
    (centred,), inverse = moments([x])
    u = (centred * inverse * gain[...]).astype(BF16)
    for i, scratch in enumerate((q_s, k_s, v_s)):
        scratch[...] = round16(mm(u, project[:, i * width : (i + 1) * width]))
    windows = n // 72
    across = windows // bias.shape[1]
    types16 = types_of(types)
    kinds[...] = kinds_of(place[0], place[1], bias.shape[1], 1, surface, row, col)

    def window(i, carry):
        first = i * TOGETHER
        places = window_rows(windows, first, TOGETHER)
        work = [(place, g, lanes, n_g) for place in places for g, (lanes, n_g) in enumerate(lane_groups(width))]
        terms = []
        for j in range(TOGETHER):
            kinds16 = kinds[pl.ds(pl.multiple_of((first + j) * 72, 8), 72), :].astype(BF16)
            terms += [mm(kinds16, t) for t in types16] * 2
        p, o = attention_forward(
            [(q_s[x[2], lanes], k_s[x[2], lanes], v_s[x[2], lanes]) for x, _, lanes, _ in work],
            [bias[x[0], x[1] // across, 0, :, 288 * g : 288 * g + n_g.stop] for x, g, _, n_g in work], terms,
        )
        for ((level, w, rows), g, lanes, n_g), a, x in zip(work, p, o):
            kept_p[level * windows + w, g, :, n_g] = a
            o_s[rows, lanes] = x
        return carry

    lax.fori_loop(0, windows // TOGETHER, window, 0, unroll=UNROLL)
    o16 = o_s[...].astype(BF16)
    kept_o[...] = o16
    out = (x + mm(o16, combine[...])).astype(BF16)
    output[...] = out
    for level in range(2):
        send_out(sel[...], out[level * n : (level + 1) * n], (sa, sb, sc), level)


def coarse_kernel(
    place, take, ctake, csel, fsel, fine, ra, rb, rc, cot, da, db, dc,
    merge_gain, merge_weight, gain, project, combine, bias, surface, types, row, col,
    output, oa, ob, oc, delta_fine, sa, sb, sc, kept_merged, kept,
    q_s, k_s, v_s, o_s, do_s, dq_s, dk_s, dv_s,
):
    n = take.shape[0]
    quarter = n // 4
    thin = fine.shape[1]
    width = combine.shape[0]
    total = n + ra.shape[1] + rb.shape[1] + rc.shape[1]
    hot = one_hot(take[...], total)
    ctotal = quarter + da.shape[1] + db.shape[1] + dc.shape[1]
    chot = one_hot(ctake[...], ctotal)
    levels, cot_levels = [], []
    for level in range(2):
        source = jnp.concatenate([fine[level * n : (level + 1) * n, :], ra[level], rb[level], rc[level]], axis=0)
        levels.append(mm(hot, source))
        o = 1 - level
        source = jnp.concatenate([cot[o * quarter : (o + 1) * quarter, :], da[o], db[o], dc[o]], axis=0)
        cot_levels.append(mm(chot, source))
    cells = [
        jnp.concatenate([x[s * quarter : (s + 1) * quarter] for x in levels], axis=0) for s in range(4)
    ]
    d = jnp.concatenate(cot_levels, axis=0)
    d16 = d.astype(BF16)
    merge_gains = [merge_gain[s : s + 1, :] for s in range(4)]
    m_centred, m_inverse = moments(cells)
    merged = [(c * m_inverse * g).astype(BF16) for c, g in zip(m_centred, merge_gains)]
    weight = [merge_weight[s * thin : (s + 1) * thin, :] for s in range(4)]
    entered = sum(mm(a, w) for a, w in zip(merged, weight))
    x = round16(entered)
    (centred,), inverse = moments([x])
    u = (centred * inverse * gain[...]).astype(BF16)
    wq, wk, wv = (project[:, i * width : (i + 1) * width] for i in range(3))
    q_s[...] = round16(mm(u, wq))
    k_s[...] = round16(mm(u, wk))
    v_s[...] = round16(mm(u, wv))
    do_s[...] = round16(mm(d16, combine[...], NT))
    windows = quarter // 72
    types16 = types_of(types)
    kinds = kinds_of(place[0], place[1], 1, 2, surface, row, col)

    places = window_rows(windows, 0, windows)
    work = [(place, g, lanes, n_g) for place in places for g, (lanes, n_g) in enumerate(lane_groups(width))]
    blocks = [(q_s[x[2], lanes], k_s[x[2], lanes], v_s[x[2], lanes]) for x, _, lanes, _ in work]
    terms = []
    for j in range(windows):
        terms += [mm(kinds[72 * j : 72 * (j + 1), :].astype(BF16), t) for t in types16] * 2
    p, o = attention_forward(blocks, [bias[x[0], 0, g, :, n_g] for x, g, _, n_g in work], terms)
    back = attention_back(blocks, p, [do_s[x[2], lanes] for x, _, lanes, _ in work])
    for ((_, _, rows), _, lanes, _), mixed, (dq, dk, dv) in zip(work, o, back):
        o_s[rows, lanes] = mixed
        dq_s[rows, lanes] = dq
        dk_s[rows, lanes] = dk
        dv_s[rows, lanes] = dv
    o16 = o_s[...].astype(BF16)
    out = (x + mm(o16, combine[...])).astype(BF16)
    output[...] = out
    for level in range(2):
        send_out(csel[...], out[level * quarter : (level + 1) * quarter], (oa, ob, oc), level)
    dq16, dk16, dv16 = dq_s[...].astype(BF16), dk_s[...].astype(BF16), dv_s[...].astype(BF16)
    delta_rolled = round16(mm(dq16, wq, NT) + mm(dk16, wk, NT) + mm(dv16, wv, NT))
    (dx,) = norm_back([centred * inverse], inverse, [gain[...]], [delta_rolled])
    delta = (d + round16(dx)).astype(BF16)
    deltas = [round16(mm(delta, w, NT)) for w in weight]
    back = norm_back([c * m_inverse for c in m_centred], m_inverse, merge_gains, deltas)
    back = [b.astype(BF16) for b in back]
    for level in range(2):
        own = jnp.concatenate([b[level * quarter : (level + 1) * quarter] for b in back], axis=0)
        delta_fine[level * n : (level + 1) * n, :] = own
        send_out(fsel[...], own, (sa, sb, sc), level)
    for s in range(4):
        kept_merged[s] = merged[s]
    for i, x in enumerate((u, dq16, dk16, dv16, o16, d16, delta)):
        kept[i] = x


def coarse_gradient_kernel(merged, kept, gradients):
    u, dq16, dk16, dv16, o16, d16, delta = (kept[i] for i in range(7))
    sums = [jnp.concatenate([mm(merged[s], delta, TN) for s in range(4)], axis=0)]
    sums += [mm(left, right, TN) for left, right in ((u, dq16), (u, dk16), (u, dv16), (o16, d16))]
    at = 0
    for block in sums:
        for j in range(block.shape[1] // 128):
            gradients[at : at + block.shape[0], :] = block[:, j * 128 : (j + 1) * 128].astype(BF16)
            at += block.shape[0]


def fine_again_kernel(kept_x, gain, project, kept_u, unit, inverse_out, q, k, v):
    width = kept_x.shape[1]
    (centred,), inverse = moments([kept_x[...].astype(F32)])
    scaled = centred * inverse
    u = (scaled * gain[...]).astype(BF16)
    kept_u[...] = u
    unit[...] = scaled
    inverse_out[...] = jnp.broadcast_to(inverse, inverse_out.shape)
    for i, out in enumerate((q, k, v)):
        out[...] = round16(mm(u, project[:, i * width : (i + 1) * width]))


def fine_backward_kernel(
    take, sel, own, ra, rb, rc, unit, inverse, q_s, k_s, v_s, kept_p, gain, project, combine,
    output, sa, sb, sc, kept,
    do_s, dq_s, dk_s, dv_s,
):
    n = take.shape[0]
    width = unit.shape[1]
    total = n + ra.shape[1] + rb.shape[1] + rc.shape[1]
    hot = one_hot(take[...], total)
    d = jnp.concatenate(
        [
            mm(hot, jnp.concatenate([own[l * n : (l + 1) * n, :], ra[l], rb[l], rc[l]], axis=0))
            for l in range(2)
        ],
        axis=0,
    )
    d16 = d.astype(BF16)
    do_s[...] = round16(mm(d16, combine[...], NT))
    windows = n // 72

    def window(i, carry):
        places = window_rows(windows, i * TOGETHER, TOGETHER)
        work = [(place, g, lanes, n_g) for place in places for g, (lanes, n_g) in enumerate(lane_groups(width))]
        back = attention_back(
            [(q_s[x[2], lanes], k_s[x[2], lanes], v_s[x[2], lanes]) for x, _, lanes, _ in work],
            [kept_p[x[0] * windows + x[1], g, :, n_g] for x, g, _, n_g in work],
            [do_s[x[2], lanes] for x, _, lanes, _ in work],
        )
        for ((_, _, rows), _, lanes, _), (dq, dk, dv) in zip(work, back):
            dq_s[rows, lanes] = dq
            dk_s[rows, lanes] = dk
            dv_s[rows, lanes] = dv
        return carry

    lax.fori_loop(0, windows // TOGETHER, window, 0, unroll=UNROLL)
    parts = [dq_s[...].astype(BF16), dk_s[...].astype(BF16), dv_s[...].astype(BF16)]
    delta_rolled = round16(
        sum(mm(a, project[:, i * width : (i + 1) * width], NT) for i, a in enumerate(parts))
    )
    (dx,) = norm_back([unit[...]], inverse[:, 0:1], [gain[...]], [delta_rolled])
    out = (d + round16(dx)).astype(BF16)
    output[...] = out
    for level in range(2):
        send_out(sel[...], out[level * n : (level + 1) * n], (sa, sb, sc), level)
    for i, x in enumerate(parts + [d16]):
        kept[i] = x


def fine_gradient_kernel(kept_u, kept_o, kept, coarse, gradients):
    width, at = kept_u.shape[1], coarse.shape[0]
    gradients[:at, :] = coarse[...]
    pieces = [mm(kept_u[...], kept[i], TN) for i in range(3)] + [mm(kept_o[...], kept[3], TN)]
    pieces = jnp.concatenate(pieces, axis=1).astype(BF16)
    for j in range(pieces.shape[1] // 128):
        gradients[at : at + width, :] = pieces[:, j * 128 : (j + 1) * 128]
        at += width
    gradients[at:, :] = jnp.zeros((gradients.shape[0] - at, 128), BF16)


def restore_kernel(take, own, ra, rb, rc, output):
    n = take.shape[0]
    hot = one_hot(take[...], n + ra.shape[1] + rb.shape[1] + rc.shape[1])
    for level in range(2):
        o = 1 - level
        source = jnp.concatenate([own[o * n : (o + 1) * n, :], ra[o], rb[o], rc[o]], axis=0)
        output[level * n : (level + 1) * n, :] = mm(hot, source).astype(BF16)


VMEM = pl.BlockSpec(memory_space=pltpu.VMEM)
SMEM = pl.BlockSpec(memory_space=pltpu.SMEM)


LIMITS = {"fine_bias": 6, "coarse_bias": 6, "fine_again": 8, "coarse_gradients": 6, "fine_gradients": 6, "restore_coarse": 4, "restore_fine": 6, "add": 4, "finish": 6}


def call(kernel, name, outs, scratch, args, smem=0, flops=10**9, limit=16, space=pltpu.VMEM, copies=0):
    limit = LIMITS.get(name, limit)
    given = pl.BlockSpec(memory_space=space)
    semaphores = [pltpu.SemaphoreType.DMA((copies,))] if copies else []
    return pl.pallas_call(
        kernel,
        name=name,
        out_shape=[jax.ShapeDtypeStruct(s, d) for s, d in outs],
        in_specs=[SMEM] * smem + [given] * (len(args) - smem),
        out_specs=[VMEM] * len(outs),
        scratch_shapes=[pltpu.VMEM(s, d) for s, d in scratch] + semaphores,
        cost_estimate=pl.CostEstimate(flops=flops, bytes_accessed=4 << 20, transcendentals=0),
        compiler_params=pltpu.CompilerParams(vmem_limit_bytes=limit << 20),
    )(*args)


def move(value, lat_step, lon_step):
    lons, lats = lax.axis_size("lon"), lax.axis_size("lat")
    if lat_step == 0:
        return lax.ppermute(value, "lon", [(s, (s + lon_step) % lons) for s in range(lons)])
    if lon_step == 0:
        return lax.ppermute(value, "lat", [(s, (s + lat_step) % lats) for s in range(lats)])
    pairs = [
        (a * lats + b, ((a + lon_step) % lons) * lats + (b + lat_step) % lats)
        for a in range(lons)
        for b in range(lats)
    ]
    return lax.ppermute(value, ("lon", "lat"), pairs)


def exchange(parts, step):
    a, b, c = parts
    return [move(a, step, 0), move(b, 0, step), move(c, step, step)]


def add_kernel(terms, repeated):
    count = terms.shape[0]

    def eight(i, total):
        return total + sum(terms[8 * i + j].astype(F32) for j in range(8))

    total = lax.fori_loop(0, count // 8, eight, jnp.zeros(terms.shape[1:], F32)).astype(BF16)

    def store(i, carry):
        for j in range(8):
            repeated[8 * i + j] = total
        return carry

    lax.fori_loop(0, count // 8, store, 0)


def summed(block, before):
    count = lax.axis_size("lon") * lax.axis_size("lat")
    block = block.reshape(count, -1, 128)
    terms = lax.all_to_all(block, ("lon", "lat"), 0, 0, tiled=True)
    terms, *before = lax.optimization_barrier((terms, *before))
    (total,) = call(add_kernel, "add", [(block.shape, BF16)], [], [terms])
    return lax.all_to_all(total, ("lon", "lat"), 0, 0, tiled=True).reshape(-1, 128), before


def finish_kernel(fine_scale, coarse_scale, sums, project1, combine1, merge, project2, combine2):
    thin, width = combine1.shape[0], combine2.shape[0]
    at = 0
    for block, lanes in ((merge, range(1)), (project2, range(3)), (combine2, range(1))):
        for i in lanes:
            for j in range(width // 128):
                rows, lane = block.shape[0], i * width + j * 128
                block[:, lane : lane + 128] = sums[at : at + rows, :].astype(F32) * coarse_scale
                at += rows
    pieces = [sums[at + j * thin : at + (j + 1) * thin, :].astype(F32) for j in range(4 * thin // 128)]
    whole = jnp.concatenate(pieces, axis=1) * fine_scale
    project1[...] = whole[:, : 3 * thin]
    combine1[...] = whole[:, 3 * thin :]


def local(
    fine_tokens, cotangent, fine_gain, fine_project, fine_combine, fine_table, fine_types,
    merge_gain, merge_weight, coarse_gain, coarse_project, coarse_combine, coarse_table,
    coarse_types, surface_type, latitude_valid, bias_index,
):
    _, rows1, cols1, d1 = fine_tokens.shape
    _, rows2, cols2, d2 = cotangent.shape
    n1, n2 = rows1 * cols1, rows2 * cols2
    h1, h2 = d1 // HEAD, d2 // HEAD
    lons, lats = lax.axis_size("lon"), lax.axis_size("lat")
    enter = Shift(rows1, cols1, 3, 6, raster(cols1), windowed(cols1), True)
    middle = Shift(rows1, cols1, 3, 6, windowed(cols1), merging(cols1), True)
    return_middle = Shift(rows1, cols1, 3, 6, merging(cols1), windowed(cols1), False)
    leave = Shift(rows1, cols1, 3, 6, windowed(cols1), raster(cols1), False)
    centre = Shift(rows2, cols2, 3, 6, raster(cols2), windowed(cols2), True)
    cleave = Shift(rows2, cols2, 3, 6, windowed(cols2), raster(cols2), False)
    fine_halo = [((2, s, d1), BF16) for s in enter.sizes]
    coarse_halo = [((2, s, d2), BF16) for s in centre.sizes]
    tokens = fine_tokens.reshape(2 * n1, d1)
    cot = cotangent.reshape(2 * n2, d2)

    halos = call(
        prepare_kernel, "prepare", fine_halo + coarse_halo,
        [(x.shape, x.dtype) for x in (enter.send, centre.send, tokens, cot)],
        [enter.send, centre.send, tokens, cot], limit=60, space=pltpu.HBM, copies=4,
    )
    token_halo = exchange(halos[:3], -1)
    cot_halo = exchange(halos[3:], -1)

    place = jnp.stack([lax.axis_index("lat"), lax.axis_index("lon"), jnp.int32(lats)]).astype(jnp.int32)
    pairs = jnp.concatenate([bias_index[:72, :72].T, bias_index[72:, 72:].T], axis=0)
    pairs = jnp.pad(pairs.reshape(48, 216), ((0, 0), (0, 40)))[:, None]

    def level_bias(name, where, table, types, level_rows, rows, cols, run):
        lists = jnp.transpose(table[0], (2, 0, 1))
        count = lists.shape[0] * lists.shape[1]
        chunks = -(-lists.shape[2] // 128)
        (bias,) = call(
            partial(bias_kernel, level_rows, surface_type.shape[0]), name,
            [((2, rows // 6, types.shape[1] // run, 72, 72 * run), F32)],
            [((pad8(count) * 144, 128), F32), ((count * chunks, 256), BF16)],
            [where, latitude_valid, pairs, lists], smem=2, flops=4 * 10**9,
        )
        t = types.T
        t = jnp.pad(jnp.concatenate([t, t, t], axis=1), ((0, 0), (0, 128 - 9)))
        order = windowed(cols)
        r, c = np.zeros((rows * cols, 1), np.int32), np.zeros((rows * cols, 1), np.int32)
        for a in range(rows):
            for b in range(cols):
                r[order(a, b), 0], c[order(a, b), 0] = a + 3, b + 6
        return bias, surface_type, t, r, c

    fine_bias = level_bias("fine_bias", place, fine_table, fine_types, 1, rows1, cols1, h1)

    token16 = lambda width: ((2 * n1, width), BF16)
    blocks1 = 2 * n1 // 72
    forward = call(
        fine_forward_kernel, "fine_forward",
        [token16(d1)] + fine_halo + [token16(d1), ((blocks1, -(-h1 // 4), 72, 288), BF16), token16(d1)],
        [((2 * n1, d1), F32)] * 4 + [((n1, 128), F32)],
        [place, enter.take, middle.send, tokens, *token_halo, fine_gain[None], fine_project, fine_combine,
         *fine_bias],
        smem=1, flops=4 * 10**9,
    )
    fine_output, kept = forward[0], forward[4:]
    halo = exchange(forward[1:4], -1)
    later, _ = lax.optimization_barrier((place, forward[1]))
    coarse_bias = level_bias("coarse_bias", later, coarse_table, coarse_types, 2, rows2, cols2, 4)

    rows = (4 * d1 + 4 * d2) * d2 // 128
    coarse = call(
        coarse_kernel, "coarse",
        [((2 * n2, d2), BF16)] + coarse_halo + [token16(d1)] + fine_halo
        + [((4, 2 * n2, d1), BF16), ((7, 2 * n2, d2), BF16)],
        [((2 * n2, d2), F32)] * 8,
        [place, middle.take, centre.take, cleave.send, return_middle.send, fine_output, *halo, cot, *cot_halo,
         merge_gain.reshape(4, d1), merge_weight, coarse_gain[None], coarse_project, coarse_combine,
         *coarse_bias],
        smem=1, flops=6 * 10**9,
    )
    delta_halo = exchange(coarse[5:8], 1)
    out_halo = exchange(coarse[1:4], 1)
    kept_x, kept_p, kept_o, after = lax.optimization_barrier((*kept, coarse[8]))
    (coarse_sums,) = call(
        coarse_gradient_kernel, "coarse_gradients", [((rows, 128), BF16)], [], [after, coarse[9]], flops=2 * 10**9,
    )
    wide = ((2 * n1, d1), F32)
    u, unit, inverse, q, k, v = call(
        fine_again_kernel, "fine_again", [token16(d1), wide, ((2 * n1, 128), F32), wide, wide, wide], [],
        [kept_x, fine_gain[None], fine_project], flops=2 * 10**9,
    )
    backward = call(
        fine_backward_kernel, "fine_backward",
        [token16(d1)] + fine_halo + [((4, 2 * n1, d1), BF16)],
        [wide] * 4,
        [return_middle.take, leave.send, coarse[4], *delta_halo, unit, inverse, q, k, v, kept_p,
         fine_gain[None], fine_project, fine_combine],
        flops=6 * 10**9,
    )
    last_halo = exchange(backward[1:4], 1)
    count = lons * lats
    chunk = pad16(-(-(rows + 4 * d1 * d1 // 128) // count))
    (sums,) = call(
        fine_gradient_kernel, "fine_gradients", [((count * chunk, 128), BF16)], [],
        [u, kept_o, backward[4], coarse_sums], flops=2 * 10**9,
    )
    sums, *out_halo = lax.optimization_barrier((sums, *out_halo))
    sums, last_halo = summed(sums, last_halo)

    (coarse_out,) = call(
        restore_kernel, "restore_coarse", [((2 * n2, d2), BF16)], [],
        [cleave.take, coarse[0], *out_halo],
    )
    count = 2 * n1 * lons * lats
    fine_scale, coarse_scale = 1.0 / math.sqrt(count), 1.0 / math.sqrt(count // 4)
    (gradient,) = call(
        restore_kernel, "restore_fine", [token16(d1)], [],
        [leave.take, backward[0], *last_halo],
    )
    gradients = call(
        partial(finish_kernel, fine_scale, coarse_scale), "finish",
        [((d1, 3 * d1), F32), ((d1, d1), F32), ((4 * d1, d2), F32), ((d2, 3 * d2), F32), ((d2, d2), F32)],
        [], [sums],
    )
    return (coarse_out.reshape(cotangent.shape), gradient.reshape(fine_tokens.shape), *gradients)


def solution(mesh):
    split = P(None, "lat", "lon", None)
    table = P(None, "lat", None, None)
    in_specs = (
        split, split, P(), P(), P(), table, P(), P(), P(), P(), P(), P(), table, P(), P(), P(), P(),
    )
    out_specs = (split, split, P(), P(), P(), P(), P())
    return jax.shard_map(local, mesh=mesh, in_specs=in_specs, out_specs=out_specs, check_vma=False)
```

```python
import math
from functools import partial

import numpy as np
import jax
import jax.numpy as jnp
from jax import lax
from jax.experimental import pallas as pl
from jax.experimental.pallas import tpu as pltpu
from jax.sharding import PartitionSpec as P

F32 = jnp.float32
BF16 = jnp.bfloat16
EPSILON = 1e-05
HEAD = 32
SCALE = HEAD ** (-0.5)
BLOCKED = -1e30
UNROLL = 2
TOGETHER = 2
NT = (((1,), (1,)), ((), ()))
TN = (((0,), (0,)), ((), ()))
NN = (((1,), (0,)), ((), ()))


def pad16(n):
    return (n + 15) // 16 * 16


class Shift:
    def __init__(self, rows, cols, dr, dc, source, target, forward):
        if forward:
            ranges = (
                (range(0, dr), range(dc, cols)),
                (range(dr, rows), range(0, dc)),
                (range(0, dr), range(0, dc)),
            )
        else:
            ranges = (
                (range(rows - dr, rows), range(0, cols - dc)),
                (range(0, rows - dr), range(cols - dc, cols)),
                (range(rows - dr, rows), range(cols - dc, cols)),
            )
        lists = [[(r, c) for r in rr for c in cc] for rr, cc in ranges]
        self.sizes = [pad16(len(x)) for x in lists]
        self.own = rows * cols
        send = []
        for x, size in zip(lists, self.sizes):
            send += [source(r, c) for r, c in x] + [0] * (size - len(x))
        self.send = np.array(send, np.int32)[:, None]
        offsets = [self.own, self.own + self.sizes[0], self.own + self.sizes[0] + self.sizes[1]]
        places = [{rc: o + n for n, rc in enumerate(x)} for x, o in zip(lists, offsets)]
        take = np.zeros((self.own, 1), np.int32)
        sign = 1 if forward else -1
        for r in range(rows):
            for c in range(cols):
                a, b = r + sign * dr, c + sign * dc
                out_row, out_col = not 0 <= a < rows, not 0 <= b < cols
                a, b = a % rows, b % cols
                if out_row or out_col:
                    which = 2 if out_row and out_col else (0 if out_row else 1)
                    place = places[which][(a, b)]
                else:
                    place = source(a, b)
                take[target(r, c), 0] = place
        self.take = take
        self.total = self.own + sum(self.sizes)


def pad8(n):
    return (n + 7) // 8 * 8


def raster(cols):
    return lambda r, c: r * cols + c


def windowed(cols):
    per_row = cols // 12
    return lambda r, c: ((r // 6) * per_row + c // 12) * 72 + (r % 6) * 12 + c % 12


def merging(cols):
    coarse = windowed(cols // 2)
    quarter = lambda rows: rows
    return lambda r, c: ((r % 2) * 2 + c % 2) * 144 + coarse(r // 2, c // 2)


def one_hot(index, width):
    lanes = lax.broadcasted_iota(jnp.int32, (index.shape[0], width), 1)
    return jnp.where(lanes == index, 1.0, 0.0).astype(BF16)


def mm(a, b, dims=NN):
    return lax.dot_general(a, b, dims, preferred_element_type=F32)


def round16(x):
    return x.astype(BF16).astype(F32)


def pick(take, total, own, parts):
    return mm(one_hot(take, total), jnp.concatenate([own] + parts, axis=0))


def head_masks(channels):
    lanes = lax.broadcasted_iota(jnp.int32, (1, channels), 1)
    return [
        jnp.where((lanes >= HEAD * h) & (lanes < HEAD * (h + 1)), 1.0, 0.0)
        for h in range(channels // HEAD)
    ]


def lane_groups(channels):
    return [
        (slice(c, min(c + 128, channels)), slice(0, 72 * ((min(c + 128, channels) - c) // HEAD)))
        for c in range(0, channels, 128)
    ]


def spread_heads(x):
    return jnp.concatenate([x * m for m in head_masks(x.shape[1])], axis=0).astype(BF16)


def fold_heads(x):
    masks = head_masks(x.shape[1])
    out = x[0:72] * masks[0]
    for h in range(1, len(masks)):
        out = out + x[72 * h : 72 * (h + 1)] * masks[h]
    return out


def attention_forward(blocks, bias, scores):
    spread = [spread_heads(q) for q, _, _ in blocks]
    x = [mm(k.astype(BF16), s, NT) * SCALE for (_, k, _), s in zip(blocks, spread)]
    x = [a + (t + b) for a, t, b in zip(x, scores, bias)]
    e = [jnp.exp(a - jnp.max(a, axis=0, keepdims=True)) for a in x]
    p = [(a * (1.0 / jnp.sum(a, axis=0, keepdims=True))).astype(BF16) for a in e]
    mixed = [mm(a, v.astype(BF16), TN) for a, (_, _, v) in zip(p, blocks)]
    return p, [fold_heads(m) for m in mixed]


def attention_back(blocks, weights, deltas):
    spread = [spread_heads(d) for d in deltas]
    dp = [mm(v.astype(BF16), d, NT) for (_, _, v), d in zip(blocks, spread)]
    dv = [mm(p, d) for p, d in zip(weights, spread)]
    ds = []
    for p16, d in zip(weights, dp):
        p = p16.astype(F32)
        pd = p * round16(d)
        ds.append(((pd - p * jnp.sum(pd, axis=0, keepdims=True)) * SCALE).astype(BF16))
    dq = [mm(d, k.astype(BF16), TN) for d, (_, k, _) in zip(ds, blocks)]
    dk = [mm(d, spread_heads(q)) for d, (q, _, _) in zip(ds, blocks)]
    return [(fold_heads(x), y, z) for x, y, z in zip(dq, dk, dv)]


def window_rows(windows, first, count):
    return [
        (level, first + i, pl.ds(pl.multiple_of((level * windows + first + i) * 72, 8), 72))
        for i in range(count)
        for level in range(2)
    ]


def moments(parts):
    count = sum(x.shape[-1] for x in parts)
    mean = sum(jnp.sum(x, axis=-1, keepdims=True) for x in parts) * (1.0 / count)
    centred = [x - mean for x in parts]
    spread = sum(jnp.sum(c * c, axis=-1, keepdims=True) for c in centred) * (1.0 / count)
    return centred, lax.rsqrt(spread + EPSILON)


def norm_back(unit, inverse, gains, deltas):
    count = sum(x.shape[-1] for x in unit)
    scaled = [d * g for d, g in zip(deltas, gains)]
    mean = sum(jnp.sum(s, axis=-1, keepdims=True) for s in scaled) * (1.0 / count)
    along = sum(jnp.sum(s * u, axis=-1, keepdims=True) for s, u in zip(scaled, unit)) * (1.0 / count)
    return [(s - mean - u * along) * inverse for s, u in zip(scaled, unit)]


def send_out(index, own, refs, level):
    rows = mm(one_hot(index, own.shape[0]), own).astype(BF16)
    at = 0
    for ref in refs:
        n = ref.shape[1]
        ref[level] = rows[at : at + n]
        at += n


def prepare_kernel(fsel, csel, tokens, cot, fa, fb, fc, ca, cb, cc, fsel_s, csel_s, tokens_s, cot_s, sems):
    copies = [
        pltpu.make_async_copy(src, dst, sems.at[i])
        for i, (src, dst) in enumerate(((fsel, fsel_s), (tokens, tokens_s), (csel, csel_s), (cot, cot_s)))
    ]
    for copy in copies:
        copy.start()
    nf, nc = tokens.shape[0] // 2, cot.shape[0] // 2
    copies[0].wait()
    copies[1].wait()
    for level in range(2):
        send_out(fsel_s[...], tokens_s[level * nf : (level + 1) * nf, :], (fa, fb, fc), level)
    copies[2].wait()
    copies[3].wait()
    for level in range(2):
        send_out(csel_s[...], cot_s[level * nc : (level + 1) * nc, :], (ca, cb, cc), level)


def bias_kernel(
    level_rows, size, place, valid, index, table, bias, raw, parts,
):
    lat, lon, lats = place[0], place[1], place[2]
    windows, heads = bias.shape[1], table.shape[0]
    run = bias.shape[4] // 72
    entries = table.shape[2]
    chunks = -(-entries // 128)
    count = windows * heads
    eights, half = count // 8, chunks // 2
    pieces = []
    for c in range(chunks):
        lanes = slice(c * 128, min(c * 128 + 128, entries))
        rows = [table[h, rw : rw + 1, lanes] for rw in range(windows) for h in range(heads)]
        piece = jnp.concatenate(rows, axis=0)
        if piece.shape[1] < 128:
            piece = jnp.concatenate([piece, jnp.zeros((count, 128 - piece.shape[1]), F32)], axis=1)
        pieces.append(piece)
    groups = [p[8 * g : 8 * g + 8] for g in range(eights) for p in pieces]
    if count % 8:
        groups += [jnp.concatenate([pieces[c][8 * eights :], pieces[c + half][8 * eights :]], axis=0) for c in range(half)]
    whole = jnp.concatenate(groups, axis=0)
    parts[:, 0:128] = whole.astype(BF16)
    parts[:, 128:256] = (whole - round16(whole)).astype(BF16)
    lanes_down = lax.broadcasted_iota(jnp.int32, (128, 256), 0)
    lower = jnp.where(lax.broadcasted_iota(jnp.int32, (8, 256), 0) >= 4, half, 0)

    def three_rows(i, carry):
        place = index[i]
        hot = jnp.where(lanes_down == (place & 127), 1.0, 0.0).astype(BF16)
        found = mm(parts[...], jnp.concatenate([hot, hot], axis=0))
        chunk = jnp.broadcast_to(place >> 7, (8, 256))

        def chosen(at, steps, chunk):
            total = jnp.zeros((8, 256), F32)
            for c in range(steps):
                total = jnp.where(chunk == c, found[at + 8 * c : at + 8 * c + 8, :], total)
            return total

        totals = [chosen(8 * chunks * g, chunks, chunk) for g in range(eights)]
        if count % 8:
            total = chosen(8 * chunks * eights, half, chunk - lower)
            totals.append(total + jnp.concatenate([total[4:], total[:4]], axis=0))
        for g, total in enumerate(totals):
            for r in range(3):
                row = jnp.concatenate([total[:, 72 * r : 72 * r + 72], jnp.zeros((8, 56), F32)], axis=1)
                raw[pl.ds(g * 1152 + 3 * i + r, 8, stride=144), :] = row
        return carry

    lax.fori_loop(0, 48, three_rows, 0, unroll=4)

    key = lax.broadcasted_iota(jnp.int32, (72, 72), 0)
    query = lax.broadcasted_iota(jnp.int32, (72, 72), 1)
    key_row = sum(jnp.where(key >= 12 * r, 1, 0) for r in range(1, 6))
    apart = jnp.where((key >= 36) != (query >= 36), 1, 0)
    rows = size // level_rows
    at_end = jnp.where(lat == lats - 1, 1, 0)
    for rw in range(windows):
        real = jnp.zeros((72, 72), jnp.int32)
        for r in range(6):
            spot = lax.rem(lat * (6 * windows) + (6 * rw + r + 3), rows) * level_rows
            here = valid[spot]
            for more in range(1, level_rows):
                here = jnp.maximum(here, valid[spot + more])
            real = jnp.where(key_row == r, here, real)
        good = (real == 1) | (key == query)
        if rw == windows - 1:
            good = good & (apart * at_end == 0)
        for level in range(2):
            for h in range(heads):
                at = (rw * heads + h) * 144 + level * 72
                bias[level, rw, h // run, :, 72 * (h % run) : 72 * (h % run + 1)] = jnp.where(
                    good, raw[at : at + 72, :][:, :72], BLOCKED
                )


def kinds_of(lat, lon, windows, level_rows, surface, row, col):
    rows, columns = surface.shape[0] // level_rows, surface.shape[1] // level_rows
    codes = surface[...].astype(F32).astype(BF16)
    tokens = row.shape[0]
    line = row[...] + lat * (6 * windows)
    line = jnp.where(line >= rows, line - rows, line) * level_rows
    spot = col[...] + lon * (12 * (tokens // 72 // windows))
    spot = jnp.where(spot >= columns, spot - columns, spot) * level_rows
    lines = mm(one_hot(line, surface.shape[0]), codes)
    lanes = lax.broadcasted_iota(jnp.int32, lines.shape, 1)
    code = jnp.sum(jnp.where(lanes == spot, lines, 0.0), axis=1, keepdims=True).astype(jnp.int32)
    lanes = lax.broadcasted_iota(jnp.int32, (tokens, 128), 1)
    return jnp.where((lanes == code) | (lanes == code + 3) | (lanes == code + 6), 1.0, 0.0)


def types_of(types):
    t = types[...]
    high = round16(t)
    middle = round16(t - high)
    lanes = lax.broadcasted_iota(jnp.int32, t.shape, 1)
    split = jnp.where(lanes < 3, high, jnp.where(lanes < 6, middle, t - high - middle))
    rows = [jnp.broadcast_to(split[h : h + 1], (72, 128)) for h in range(t.shape[0])]
    return [jnp.concatenate(rows[h : h + 4], axis=0).T.astype(BF16) for h in range(0, len(rows), 4)]


def fine_forward_kernel(
    place, take, sel, tokens, ra, rb, rc, gain, project, combine, bias, surface, types, row, col,
    output, sa, sb, sc, kept_x, kept_p, kept_o,
    q_s, k_s, v_s, o_s, kinds,
):
    n = take.shape[0]
    width = tokens.shape[1]
    total = n + ra.shape[1] + rb.shape[1] + rc.shape[1]
    hot = one_hot(take[...], total)
    rolled = []
    for level in range(2):
        o = 1 - level
        source = jnp.concatenate([tokens[o * n : (o + 1) * n, :], ra[o], rb[o], rc[o]], axis=0)
        rolled.append(mm(hot, source))
    x = jnp.concatenate(rolled, axis=0)
    kept_x[...] = x.astype(BF16)
    (centred,), inverse = moments([x])
    u = (centred * inverse * gain[...]).astype(BF16)
    for i, scratch in enumerate((q_s, k_s, v_s)):
        scratch[...] = round16(mm(u, project[:, i * width : (i + 1) * width]))
    windows = n // 72
    across = windows // bias.shape[1]
    types16 = types_of(types)
    kinds[...] = kinds_of(place[0], place[1], bias.shape[1], 1, surface, row, col)

    def window(i, carry):
        first = i * TOGETHER
        places = window_rows(windows, first, TOGETHER)
        work = [(place, g, lanes, n_g) for place in places for g, (lanes, n_g) in enumerate(lane_groups(width))]
        terms = []
        for j in range(TOGETHER):
            kinds16 = kinds[pl.ds(pl.multiple_of((first + j) * 72, 8), 72), :].astype(BF16)
            terms += [mm(kinds16, t) for t in types16] * 2
        p, o = attention_forward(
            [(q_s[x[2], lanes], k_s[x[2], lanes], v_s[x[2], lanes]) for x, _, lanes, _ in work],
            [bias[x[0], x[1] // across, 0, :, 288 * g : 288 * g + n_g.stop] for x, g, _, n_g in work], terms,
        )
        for ((level, w, rows), g, lanes, n_g), a, x in zip(work, p, o):
            kept_p[level * windows + w, g, :, n_g] = a
            o_s[rows, lanes] = x
        return carry

    lax.fori_loop(0, windows // TOGETHER, window, 0, unroll=UNROLL)
    o16 = o_s[...].astype(BF16)
    kept_o[...] = o16
    out = (x + mm(o16, combine[...])).astype(BF16)
    output[...] = out
    for level in range(2):
        send_out(sel[...], out[level * n : (level + 1) * n], (sa, sb, sc), level)


def coarse_kernel(
    place, take, ctake, csel, fsel, fine, ra, rb, rc, cot, da, db, dc,
    merge_gain, merge_weight, gain, project, combine, bias, surface, types, row, col,
    output, oa, ob, oc, delta_fine, sa, sb, sc, kept_merged, kept,
    q_s, k_s, v_s, o_s, do_s, dq_s, dk_s, dv_s,
):
    n = take.shape[0]
    quarter = n // 4
    thin = fine.shape[1]
    width = combine.shape[0]
    total = n + ra.shape[1] + rb.shape[1] + rc.shape[1]
    hot = one_hot(take[...], total)
    ctotal = quarter + da.shape[1] + db.shape[1] + dc.shape[1]
    chot = one_hot(ctake[...], ctotal)
    levels, cot_levels = [], []
    for level in range(2):
        source = jnp.concatenate([fine[level * n : (level + 1) * n, :], ra[level], rb[level], rc[level]], axis=0)
        levels.append(mm(hot, source))
        o = 1 - level
        source = jnp.concatenate([cot[o * quarter : (o + 1) * quarter, :], da[o], db[o], dc[o]], axis=0)
        cot_levels.append(mm(chot, source))
    cells = [
        jnp.concatenate([x[s * quarter : (s + 1) * quarter] for x in levels], axis=0) for s in range(4)
    ]
    d = jnp.concatenate(cot_levels, axis=0)
    d16 = d.astype(BF16)
    merge_gains = [merge_gain[s : s + 1, :] for s in range(4)]
    m_centred, m_inverse = moments(cells)
    merged = [(c * m_inverse * g).astype(BF16) for c, g in zip(m_centred, merge_gains)]
    weight = [merge_weight[s * thin : (s + 1) * thin, :] for s in range(4)]
    entered = sum(mm(a, w) for a, w in zip(merged, weight))
    x = round16(entered)
    (centred,), inverse = moments([x])
    u = (centred * inverse * gain[...]).astype(BF16)
    wq, wk, wv = (project[:, i * width : (i + 1) * width] for i in range(3))
    q_s[...] = round16(mm(u, wq))
    k_s[...] = round16(mm(u, wk))
    v_s[...] = round16(mm(u, wv))
    do_s[...] = round16(mm(d16, combine[...], NT))
    windows = quarter // 72
    types16 = types_of(types)
    kinds = kinds_of(place[0], place[1], 1, 2, surface, row, col)

    places = window_rows(windows, 0, windows)
    work = [(place, g, lanes, n_g) for place in places for g, (lanes, n_g) in enumerate(lane_groups(width))]
    blocks = [(q_s[x[2], lanes], k_s[x[2], lanes], v_s[x[2], lanes]) for x, _, lanes, _ in work]
    terms = []
    for j in range(windows):
        terms += [mm(kinds[72 * j : 72 * (j + 1), :].astype(BF16), t) for t in types16] * 2
    p, o = attention_forward(blocks, [bias[x[0], 0, g, :, n_g] for x, g, _, n_g in work], terms)
    back = attention_back(blocks, p, [do_s[x[2], lanes] for x, _, lanes, _ in work])
    for ((_, _, rows), _, lanes, _), mixed, (dq, dk, dv) in zip(work, o, back):
        o_s[rows, lanes] = mixed
        dq_s[rows, lanes] = dq
        dk_s[rows, lanes] = dk
        dv_s[rows, lanes] = dv
    o16 = o_s[...].astype(BF16)
    out = (x + mm(o16, combine[...])).astype(BF16)
    output[...] = out
    for level in range(2):
        send_out(csel[...], out[level * quarter : (level + 1) * quarter], (oa, ob, oc), level)
    dq16, dk16, dv16 = dq_s[...].astype(BF16), dk_s[...].astype(BF16), dv_s[...].astype(BF16)
    delta_rolled = round16(mm(dq16, wq, NT) + mm(dk16, wk, NT) + mm(dv16, wv, NT))
    (dx,) = norm_back([centred * inverse], inverse, [gain[...]], [delta_rolled])
    delta = (d + round16(dx)).astype(BF16)
    deltas = [round16(mm(delta, w, NT)) for w in weight]
    back = norm_back([c * m_inverse for c in m_centred], m_inverse, merge_gains, deltas)
    back = [b.astype(BF16) for b in back]
    for level in range(2):
        own = jnp.concatenate([b[level * quarter : (level + 1) * quarter] for b in back], axis=0)
        delta_fine[level * n : (level + 1) * n, :] = own
        send_out(fsel[...], own, (sa, sb, sc), level)
    for s in range(4):
        kept_merged[s] = merged[s]
    for i, x in enumerate((u, dq16, dk16, dv16, o16, d16, delta)):
        kept[i] = x


def coarse_gradient_kernel(merged, kept, gradients):
    u, dq16, dk16, dv16, o16, d16, delta = (kept[i] for i in range(7))
    sums = [jnp.concatenate([mm(merged[s], delta, TN) for s in range(4)], axis=0)]
    sums += [mm(left, right, TN) for left, right in ((u, dq16), (u, dk16), (u, dv16), (o16, d16))]
    at = 0
    for block in sums:
        for j in range(block.shape[1] // 128):
            gradients[at : at + block.shape[0], :] = block[:, j * 128 : (j + 1) * 128].astype(BF16)
            at += block.shape[0]


def fine_again_kernel(kept_x, gain, project, kept_u, unit, inverse_out, q, k, v):
    width = kept_x.shape[1]
    (centred,), inverse = moments([kept_x[...].astype(F32)])
    scaled = centred * inverse
    u = (scaled * gain[...]).astype(BF16)
    kept_u[...] = u
    unit[...] = scaled
    inverse_out[...] = jnp.broadcast_to(inverse, inverse_out.shape)
    for i, out in enumerate((q, k, v)):
        out[...] = round16(mm(u, project[:, i * width : (i + 1) * width]))


def fine_backward_kernel(
    take, sel, own, ra, rb, rc, unit, inverse, q_s, k_s, v_s, kept_p, gain, project, combine,
    output, sa, sb, sc, kept,
    do_s, dq_s, dk_s, dv_s,
):
    n = take.shape[0]
    width = unit.shape[1]
    total = n + ra.shape[1] + rb.shape[1] + rc.shape[1]
    hot = one_hot(take[...], total)
    d = jnp.concatenate(
        [
            mm(hot, jnp.concatenate([own[l * n : (l + 1) * n, :], ra[l], rb[l], rc[l]], axis=0))
            for l in range(2)
        ],
        axis=0,
    )
    d16 = d.astype(BF16)
    do_s[...] = round16(mm(d16, combine[...], NT))
    windows = n // 72

    def window(i, carry):
        places = window_rows(windows, i * TOGETHER, TOGETHER)
        work = [(place, g, lanes, n_g) for place in places for g, (lanes, n_g) in enumerate(lane_groups(width))]
        back = attention_back(
            [(q_s[x[2], lanes], k_s[x[2], lanes], v_s[x[2], lanes]) for x, _, lanes, _ in work],
            [kept_p[x[0] * windows + x[1], g, :, n_g] for x, g, _, n_g in work],
            [do_s[x[2], lanes] for x, _, lanes, _ in work],
        )
        for ((_, _, rows), _, lanes, _), (dq, dk, dv) in zip(work, back):
            dq_s[rows, lanes] = dq
            dk_s[rows, lanes] = dk
            dv_s[rows, lanes] = dv
        return carry

    lax.fori_loop(0, windows // TOGETHER, window, 0, unroll=UNROLL)
    parts = [dq_s[...].astype(BF16), dk_s[...].astype(BF16), dv_s[...].astype(BF16)]
    delta_rolled = round16(
        sum(mm(a, project[:, i * width : (i + 1) * width], NT) for i, a in enumerate(parts))
    )
    (dx,) = norm_back([unit[...]], inverse[:, 0:1], [gain[...]], [delta_rolled])
    out = (d + round16(dx)).astype(BF16)
    output[...] = out
    for level in range(2):
        send_out(sel[...], out[level * n : (level + 1) * n], (sa, sb, sc), level)
    for i, x in enumerate(parts + [d16]):
        kept[i] = x


def fine_gradient_kernel(kept_u, kept_o, kept, coarse, gradients, rows, sems):
    width = kept_u.shape[1]
    pieces = [mm(kept_u[...], kept[i], TN) for i in range(3)] + [mm(kept_o[...], kept[3], TN)]
    pieces = jnp.concatenate(pieces, axis=1).astype(BF16)
    count = pieces.shape[1] // 128
    for j in range(count):
        rows[j * width : (j + 1) * width, :] = pieces[:, j * 128 : (j + 1) * 128]
    rows[count * width :, :] = jnp.zeros((rows.shape[0] - count * width, 128), BF16)
    at = gradients.shape[0] - rows.shape[0]
    copy = pltpu.make_async_copy(rows, gradients.at[at:, :], sems.at[0])
    copy.start()
    copy.wait()


def restore_kernel(take, own, ra, rb, rc, output):
    n = take.shape[0]
    hot = one_hot(take[...], n + ra.shape[1] + rb.shape[1] + rc.shape[1])
    for level in range(2):
        o = 1 - level
        source = jnp.concatenate([own[o * n : (o + 1) * n, :], ra[o], rb[o], rc[o]], axis=0)
        output[level * n : (level + 1) * n, :] = mm(hot, source).astype(BF16)


VMEM = pl.BlockSpec(memory_space=pltpu.VMEM)
SMEM = pl.BlockSpec(memory_space=pltpu.SMEM)


LIMITS = {"fine_bias": 6, "coarse_bias": 6, "fine_again": 8, "coarse_gradients": 6, "fine_gradients": 6, "restore_coarse": 4, "restore_fine": 6, "add": 4, "finish": 6}


def call(kernel, name, outs, scratch, args, smem=0, flops=10**9, limit=16, space=pltpu.VMEM, copies=0):
    limit = LIMITS.get(name, limit)
    given = pl.BlockSpec(memory_space=space)
    semaphores = [pltpu.SemaphoreType.DMA((copies,))] if copies else []
    return pl.pallas_call(
        kernel,
        name=name,
        out_shape=[jax.ShapeDtypeStruct(s, d) for s, d in outs],
        in_specs=[SMEM] * smem + [given] * (len(args) - smem),
        out_specs=[VMEM] * len(outs),
        scratch_shapes=[pltpu.VMEM(s, d) for s, d in scratch] + semaphores,
        cost_estimate=pl.CostEstimate(flops=flops, bytes_accessed=4 << 20, transcendentals=0),
        compiler_params=pltpu.CompilerParams(vmem_limit_bytes=limit << 20),
    )(*args)


def move(value, lat_step, lon_step):
    lons, lats = lax.axis_size("lon"), lax.axis_size("lat")
    if lat_step == 0:
        return lax.ppermute(value, "lon", [(s, (s + lon_step) % lons) for s in range(lons)])
    if lon_step == 0:
        return lax.ppermute(value, "lat", [(s, (s + lat_step) % lats) for s in range(lats)])
    pairs = [
        (a * lats + b, ((a + lon_step) % lons) * lats + (b + lat_step) % lats)
        for a in range(lons)
        for b in range(lats)
    ]
    return lax.ppermute(value, ("lon", "lat"), pairs)


def exchange(parts, step):
    a, b, c = parts
    return [move(a, step, 0), move(b, 0, step), move(c, step, step)]


def add_kernel(terms, repeated):
    count = terms.shape[0]

    def eight(i, total):
        return total + sum(terms[8 * i + j].astype(F32) for j in range(8))

    total = lax.fori_loop(0, count // 8, eight, jnp.zeros(terms.shape[1:], F32)).astype(BF16)

    def store(i, carry):
        for j in range(8):
            repeated[8 * i + j] = total
        return carry

    lax.fori_loop(0, count // 8, store, 0)


def summed(block, before):
    count = lax.axis_size("lon") * lax.axis_size("lat")
    block = block.reshape(count, -1, 128)
    terms = lax.all_to_all(block, ("lon", "lat"), 0, 0, tiled=True)
    terms, *before = lax.optimization_barrier((terms, *before))
    (total,) = call(add_kernel, "add", [(block.shape, BF16)], [], [terms])
    return lax.all_to_all(total, ("lon", "lat"), 0, 0, tiled=True).reshape(-1, 128), before


def finish_kernel(fine_scale, coarse_scale, sums, project1, combine1, merge, project2, combine2):
    thin, width = combine1.shape[0], combine2.shape[0]
    at = 0
    for block, lanes in ((merge, range(1)), (project2, range(3)), (combine2, range(1))):
        for i in lanes:
            for j in range(width // 128):
                rows, lane = block.shape[0], i * width + j * 128
                block[:, lane : lane + 128] = sums[at : at + rows, :].astype(F32) * coarse_scale
                at += rows
    pieces = [sums[at + j * thin : at + (j + 1) * thin, :].astype(F32) for j in range(4 * thin // 128)]
    whole = jnp.concatenate(pieces, axis=1) * fine_scale
    project1[...] = whole[:, : 3 * thin]
    combine1[...] = whole[:, 3 * thin :]


def local(
    fine_tokens, cotangent, fine_gain, fine_project, fine_combine, fine_table, fine_types,
    merge_gain, merge_weight, coarse_gain, coarse_project, coarse_combine, coarse_table,
    coarse_types, surface_type, latitude_valid, bias_index,
):
    _, rows1, cols1, d1 = fine_tokens.shape
    _, rows2, cols2, d2 = cotangent.shape
    n1, n2 = rows1 * cols1, rows2 * cols2
    h1, h2 = d1 // HEAD, d2 // HEAD
    lons, lats = lax.axis_size("lon"), lax.axis_size("lat")
    enter = Shift(rows1, cols1, 3, 6, raster(cols1), windowed(cols1), True)
    middle = Shift(rows1, cols1, 3, 6, windowed(cols1), merging(cols1), True)
    return_middle = Shift(rows1, cols1, 3, 6, merging(cols1), windowed(cols1), False)
    leave = Shift(rows1, cols1, 3, 6, windowed(cols1), raster(cols1), False)
    centre = Shift(rows2, cols2, 3, 6, raster(cols2), windowed(cols2), True)
    cleave = Shift(rows2, cols2, 3, 6, windowed(cols2), raster(cols2), False)
    fine_halo = [((2, s, d1), BF16) for s in enter.sizes]
    coarse_halo = [((2, s, d2), BF16) for s in centre.sizes]
    tokens = fine_tokens.reshape(2 * n1, d1)
    cot = cotangent.reshape(2 * n2, d2)

    halos = call(
        prepare_kernel, "prepare", fine_halo + coarse_halo,
        [(x.shape, x.dtype) for x in (enter.send, centre.send, tokens, cot)],
        [enter.send, centre.send, tokens, cot], limit=60, space=pltpu.HBM, copies=4,
    )
    token_halo = exchange(halos[:3], -1)
    cot_halo = exchange(halos[3:], -1)

    place = jnp.stack([lax.axis_index("lat"), lax.axis_index("lon"), jnp.int32(lats)]).astype(jnp.int32)
    pairs = jnp.concatenate([bias_index[:72, :72].T, bias_index[72:, 72:].T], axis=0)
    pairs = jnp.pad(pairs.reshape(48, 216), ((0, 0), (0, 40)))[:, None]

    def level_bias(name, where, table, types, level_rows, rows, cols, run):
        lists = jnp.transpose(table[0], (2, 0, 1))
        count = lists.shape[0] * lists.shape[1]
        chunks = -(-lists.shape[2] // 128)
        (bias,) = call(
            partial(bias_kernel, level_rows, surface_type.shape[0]), name,
            [((2, rows // 6, types.shape[1] // run, 72, 72 * run), F32)],
            [((pad8(count) * 144, 128), F32), ((count * chunks, 256), BF16)],
            [where, latitude_valid, pairs, lists], smem=2, flops=4 * 10**9,
        )
        t = types.T
        t = jnp.pad(jnp.concatenate([t, t, t], axis=1), ((0, 0), (0, 128 - 9)))
        order = windowed(cols)
        r, c = np.zeros((rows * cols, 1), np.int32), np.zeros((rows * cols, 1), np.int32)
        for a in range(rows):
            for b in range(cols):
                r[order(a, b), 0], c[order(a, b), 0] = a + 3, b + 6
        return bias, surface_type, t, r, c

    fine_bias = level_bias("fine_bias", place, fine_table, fine_types, 1, rows1, cols1, h1)

    token16 = lambda width: ((2 * n1, width), BF16)
    blocks1 = 2 * n1 // 72
    forward = call(
        fine_forward_kernel, "fine_forward",
        [token16(d1)] + fine_halo + [token16(d1), ((blocks1, -(-h1 // 4), 72, 288), BF16), token16(d1)],
        [((2 * n1, d1), F32)] * 4 + [((n1, 128), F32)],
        [place, enter.take, middle.send, tokens, *token_halo, fine_gain[None], fine_project, fine_combine,
         *fine_bias],
        smem=1, flops=4 * 10**9,
    )
    fine_output, kept = forward[0], forward[4:]
    halo = exchange(forward[1:4], -1)
    later, _ = lax.optimization_barrier((place, forward[1]))
    coarse_bias = level_bias("coarse_bias", later, coarse_table, coarse_types, 2, rows2, cols2, 4)

    rows = (4 * d1 + 4 * d2) * d2 // 128
    coarse = call(
        coarse_kernel, "coarse",
        [((2 * n2, d2), BF16)] + coarse_halo + [token16(d1)] + fine_halo
        + [((4, 2 * n2, d1), BF16), ((7, 2 * n2, d2), BF16)],
        [((2 * n2, d2), F32)] * 8,
        [place, middle.take, centre.take, cleave.send, return_middle.send, fine_output, *halo, cot, *cot_halo,
         merge_gain.reshape(4, d1), merge_weight, coarse_gain[None], coarse_project, coarse_combine,
         *coarse_bias],
        smem=1, flops=6 * 10**9,
    )
    delta_halo = exchange(coarse[5:8], 1)
    out_halo = exchange(coarse[1:4], 1)
    kept_x, kept_p, kept_o, after = lax.optimization_barrier((*kept, coarse[8]))
    count = lons * lats
    chunk = pad16(-(-(rows + 4 * d1 * d1 // 128) // count))
    (coarse_sums,) = call(
        coarse_gradient_kernel, "coarse_gradients", [((count * chunk, 128), BF16)], [], [after, coarse[9]],
        flops=2 * 10**9,
    )
    wide = ((2 * n1, d1), F32)
    u, unit, inverse, q, k, v = call(
        fine_again_kernel, "fine_again", [token16(d1), wide, ((2 * n1, 128), F32), wide, wide, wide], [],
        [kept_x, fine_gain[None], fine_project], flops=2 * 10**9,
    )
    backward = call(
        fine_backward_kernel, "fine_backward",
        [token16(d1)] + fine_halo + [((4, 2 * n1, d1), BF16)],
        [wide] * 4,
        [return_middle.take, leave.send, coarse[4], *delta_halo, unit, inverse, q, k, v, kept_p,
         fine_gain[None], fine_project, fine_combine],
        flops=6 * 10**9,
    )
    last_halo = exchange(backward[1:4], 1)
    anywhere = pl.BlockSpec(memory_space=pl.ANY)
    sums = pl.pallas_call(
        fine_gradient_kernel,
        name="fine_gradients",
        out_shape=jax.ShapeDtypeStruct(coarse_sums.shape, BF16),
        in_specs=[VMEM] * 3 + [anywhere],
        out_specs=anywhere,
        scratch_shapes=[pltpu.VMEM((count * chunk - rows, 128), BF16), pltpu.SemaphoreType.DMA((1,))],
        input_output_aliases={3: 0},
        cost_estimate=pl.CostEstimate(flops=2 * 10**9, bytes_accessed=4 << 20, transcendentals=0),
        compiler_params=pltpu.CompilerParams(vmem_limit_bytes=6 << 20),
    )(u, kept_o, backward[4], coarse_sums)
    sums, *out_halo = lax.optimization_barrier((sums, *out_halo))
    sums, last_halo = summed(sums, last_halo)

    (coarse_out,) = call(
        restore_kernel, "restore_coarse", [((2 * n2, d2), BF16)], [],
        [cleave.take, coarse[0], *out_halo],
    )
    count = 2 * n1 * lons * lats
    fine_scale, coarse_scale = 1.0 / math.sqrt(count), 1.0 / math.sqrt(count // 4)
    (gradient,) = call(
        restore_kernel, "restore_fine", [token16(d1)], [],
        [leave.take, backward[0], *last_halo],
    )
    gradients = call(
        partial(finish_kernel, fine_scale, coarse_scale), "finish",
        [((d1, 3 * d1), F32), ((d1, d1), F32), ((4 * d1, d2), F32), ((d2, 3 * d2), F32), ((d2, d2), F32)],
        [], [sums],
    )
    return (coarse_out.reshape(cotangent.shape), gradient.reshape(fine_tokens.shape), *gradients)


def solution(mesh):
    split = P(None, "lat", "lon", None)
    table = P(None, "lat", None, None)
    in_specs = (
        split, split, P(), P(), P(), table, P(), P(), P(), P(), P(), P(), table, P(), P(), P(), P(),
    )
    out_specs = (split, split, P(), P(), P(), P(), P())
    return jax.shard_map(local, mesh=mesh, in_specs=in_specs, out_specs=out_specs, check_vma=False)
```
